32 devices in a mesh: dp: 4 (over x, core), mp: 8 (over z, y).
Axes of the slice: x: 2, y: 2, z: 4, core: 2. Of those that a mesh axis runs over, the one named last changes fastest.
Arguments:
- acts: bfloat16 [512, 8192], P('dp', 'mp'), may hold values from -6 to 6
- grad_out: bfloat16 [512, 7168], P('dp', 'mp'), may hold values from -6 to 6
- values: bfloat16 [56, 20, 128, 128], P('mp', None, 'dp'), may hold values from -0.125 to 0.125
- block_rows: int32 [56, 20], P('mp'), may hold values from 0 to 63, as said below
- block_count: int32 [56], P('mp'), may hold values from 12 to 20, as said below
Outputs:
- hidden_out: bfloat16 [512, 7168], P('dp', 'mp')
- grad_acts: bfloat16 [512, 8192], P('dp', 'mp')
- grad_values: float32 [56, 20, 128, 128], P('mp', None, 'dp')
The draws below stay inside these ranges and needn't reach their ends.
Inputs may be any that keep to these rules, and one draw needn't show every extreme that they name: `block_rows`: the live slots of a block column name distinct block rows; the first ones follow a butterfly pattern around block row c % 64. Slots at or after block_count are ignored. `block_count`: some block column has all 20 slots live.
All inputs are finite; a program needn't handle non-finite values.
Results may differ from the reference program's by a relative error of at most 0.02.
Values may be sent and summed in bfloat16 or wider, within the bound.
A program may use at most 128 MiB of HBM per device.

```python
import jax
import jax.numpy as jnp
from jax import lax

D = 8192
BLK = 128
CB_DEV = 7
KMAX = 20
KMIN = 12
NCB = 56
FF = 7168
TOKENS = 512
N_MP = 8


def draw_block_rows(key, part):
    key = jax.random.fold_in(key, 11)
    row_blocks = D // BLK
    columns = jnp.arange(NCB, dtype=jnp.int32)[:, None]
    positions = jnp.arange(row_blocks, dtype=jnp.int32)[None, :]
    flipped = jnp.bitwise_xor(columns % row_blocks, positions)
    butterfly = jnp.bitwise_and(flipped, flipped - 1) == 0
    noise = jax.random.randint(key, (NCB, row_blocks), 0, 2 ** 20, dtype=jnp.int32)
    scores = jnp.where(butterfly, 2 ** 27, 0) + noise * row_blocks + positions
    order = jnp.argsort(-scores, axis=1, stable=True)
    return order[:, :KMAX].astype(jnp.int32)


def draw_block_count(key, part):
    key = jax.random.fold_in(key, 23)
    first, second = jax.random.split(key)
    counts = jax.random.randint(first, (NCB,), KMIN, KMAX + 1, dtype=jnp.int32)
    fullest = jax.random.randint(second, (), 0, NCB, dtype=jnp.int32)
    return counts.at[fullest].set(KMAX).astype(jnp.int32)


def steps_of(own_key, dims, cuts, smallest, top_value):
    def one(axis_at, shards_of):
        heights = jax.random.uniform(jax.random.fold_in(jax.random.fold_in(own_key, 6), axis_at), (shards_of,), jnp.float32, smallest / len(cuts), top_value / len(cuts))
        return jnp.repeat(jnp.exp(heights), dims[axis_at] // shards_of).reshape((-1,) + (1,) * (len(dims) - axis_at - 1))

    factor_of = one(*cuts[0])
    for cut in cuts[1:]:
        factor_of = factor_of * one(*cut)
    return factor_of


def scatter_about(stream_key, dims, width, most, shards=(), kind=jnp.bfloat16):
    values = jax.random.normal(stream_key, dims, jnp.float32) * width
    if len(shards) > 0:
        values = steps_of(stream_key, dims, shards, -0.22, 0.18) * values
    return jnp.clip(values, min=-most, max=most).astype(kind)


def setup_inputs(seed: int = 0) -> dict:
    streams_of = jax.random.split(jax.random.key(seed), 6)
    return {
        "acts": scatter_about(streams_of[0], (TOKENS, D), 1.0, 6.0, ((0, 4), (1, 8))),
        "grad_out": scatter_about(streams_of[1], (TOKENS, FF), 1.0, 6.0, ((0, 4), (1, 8))),
        "values": scatter_about(streams_of[2], (NCB, KMAX, BLK, BLK), (KMAX * BLK) ** -0.5, 0.125, ((0, 8), (2, 4))),
        "block_rows": draw_block_rows(jax.random.fold_in(streams_of[5], 71), 0),
        "block_count": draw_block_count(jax.random.fold_in(streams_of[5], 71), 0),
    }


def reference(acts, grad_out, values, block_rows, block_count):
    row_blocks = D // BLK
    blocked = acts.reshape(TOKENS, row_blocks, BLK).astype(jnp.float32)
    grad_blocks = grad_out.reshape(TOKENS, NCB, BLK).astype(jnp.float32)
    slot_live = jnp.arange(KMAX, dtype=jnp.int32)[None, :] < block_count[:, None]
    masked = jnp.where(slot_live[:, :, None, None], values.astype(jnp.float32), jnp.zeros((), jnp.float32))

    def per_column(column):
        rows = block_rows[column]
        picked = jnp.take(blocked, rows, axis=1)
        upstream = grad_blocks[:, column]
        produced = jnp.einsum("tki,kij->tj", picked, masked[column])
        weight_grad = jnp.einsum("tki,tj->kij", picked, upstream)
        weight_grad = jnp.where(slot_live[column][:, None, None], weight_grad, jnp.zeros((), jnp.float32))
        return produced, weight_grad

    produced, grad_values = lax.map(per_column, jnp.arange(NCB, dtype=jnp.int32))
    hidden_out = jnp.transpose(produced, (1, 0, 2)).reshape(TOKENS, NCB * BLK).astype(jnp.bfloat16)

    def per_group(total, group):
        def add_column(offset, partial_value):
            column = group * CB_DEV + offset
            rows = block_rows[column]
            contrib = jnp.einsum("tj,kij->tki", grad_blocks[:, column], masked[column])
            return partial_value.at[:, rows].add(contrib)

        partial_value = lax.fori_loop(0, CB_DEV, add_column, jnp.zeros((TOKENS, row_blocks, BLK), jnp.float32))
        rounded = lax.optimization_barrier(partial_value.astype(jnp.bfloat16)).astype(jnp.float32)
        return total + rounded, None

    total, unused = lax.scan(per_group, jnp.zeros((TOKENS, row_blocks, BLK), jnp.float32), jnp.arange(N_MP, dtype=jnp.int32))
    grad_acts = total.reshape(TOKENS, D).astype(jnp.bfloat16)
    return hidden_out, grad_acts, grad_values
```

```python
import functools

import jax
import jax.numpy as jnp
from jax import lax
from jax.experimental import pallas as pl
from jax.experimental.pallas import tpu as pltpu
from jax.sharding import PartitionSpec as P

MESH = pl.DeviceIdType.MESH
BF16 = jnp.bfloat16
F32 = jnp.float32
N_Z = 4


def select(rows_in, lanes, width, shift):
    src = lax.broadcasted_iota(jnp.int32, (rows_in, lanes), 0)
    dst = lax.broadcasted_iota(jnp.int32, (rows_in, lanes), 1)
    hit = src == (dst // width) * 128 + shift + dst % width
    return jnp.where(hit, 1.0, 0.0).astype(BF16)


def kernel(
    nd, nm,
    acts_ref, gout_ref, w,
    hid_out, ga_out, flip, gall,
    perm, act, part, ry, rz, hid, hsend, hrecv, tot, garecv,
    aa_s, aa_r, go_s, go_r, az_s, az_r, ay_s, ay_r,
    py_s, py_r, pz_s, pz_r, hd_s, hd_r, ga_s, ga_r,
):
    nz = N_Z
    ny = nm // nz
    d = lax.axis_index("dp")
    m = lax.axis_index("mp")
    z = m // ny
    y = m % ny
    tok, local = acts_ref.shape
    ff = gout_ref.shape[1]
    blk = 128
    feat = act.shape[3]
    local_blocks = local // blk
    width = feat // local_blocks
    group = min(local_blocks, blk // width)
    gw = group * width
    n_group = local_blocks // group

    def dpeer(o):
        return (lax.rem(d + o, nd), m)

    def mpeer(zz, yy):
        return (d, zz * ny + yy)

    def zo(o):
        return lax.rem(z + o + nz, nz)

    def yo(o):
        return lax.rem(y + o + ny, ny)

    def rcopy(src, dst, ss, rs, dev):
        return pltpu.make_async_remote_copy(
            src_ref=src, dst_ref=dst, send_sem=ss, recv_sem=rs, device_id=dev, device_id_type=MESH
        )

    barrier = pltpu.get_barrier_semaphore()
    peers = [dpeer(o) for o in range(1, nd)]
    peers += [mpeer(zo(o), y) for o in range(1, nz)]
    peers += [mpeer(z, yo(b)) for b in range(1, ny)]
    for peer in peers:
        pl.semaphore_signal(barrier, inc=1, device_id=peer, device_id_type=MESH)

    for dd in range(nd):
        pick = select(group * blk, gw, width, dd * width)
        for q in range(n_group):
            got = jnp.dot(
                acts_ref[:, q * group * blk:(q + 1) * group * blk], pick, preferred_element_type=F32
            )
            perm[dd, :, q * gw:(q + 1) * gw] = got.astype(BF16)

    pl.semaphore_wait(barrier, len(peers))

    acts_sent = []
    for o in range(1, nd):
        c = rcopy(perm.at[lax.rem(d + o, nd)], act.at[m, d], aa_s.at[o], aa_r.at[o], dpeer(o))
        c.start()
        acts_sent.append(c)
    gout_sent = []
    for o in range(1, nd):
        c = rcopy(gout_ref, gall.at[d], go_s.at[o], go_r.at[o], dpeer(o))
        c.start()
        gout_sent.append(c)
    act[m, d] = perm[d]
    gall[d] = gout_ref[...]

    for c in acts_sent:
        c.wait_recv()

    sends = []
    for o in range(1, nz):
        c = rcopy(act.at[m], act.at[m], az_s.at[o], az_r.at[o], mpeer(zo(o), y))
        c.start()
        sends.append(c)

    def spread(s):
        chunk = zo(-s) * ny + y
        for b in range(1, ny):
            c = rcopy(act.at[chunk], act.at[chunk], ay_s.at[s, b], ay_r.at[s, b], mpeer(z, yo(b)))
            c.start()
            sends.append(c)

    spread(0)

    for c in gout_sent:
        c.wait_recv()

    def weights(mm):
        return w[pl.ds(pl.multiple_of(mm * feat, feat), feat), :].astype(BF16)

    def partial(mm):
        wm = weights(mm)

        @pl.loop(0, nd)
        def _(t):
            part[mm, t] = lax.dot_general(
                gall[t], wm, (((1,), (1,)), ((), ())), preferred_element_type=F32
            ).astype(BF16)

    for a in range(1, nz + 1):
        zt = zo(a % nz)
        for b in range(1, ny):
            mm = zt * ny + yo(b)
            partial(mm)
            c = rcopy(part.at[mm], ry.at[a - 1, b - 1], py_s.at[a - 1, b], py_r.at[a - 1, b], mpeer(z, yo(b)))
            c.start()
            sends.append(c)
        if a < nz:
            rcopy(act.at[m], act.at[m], az_s.at[a], az_r.at[a], mpeer(zo(a), y)).wait_recv()
            spread(a)
        partial(zt * ny + y)

    hid[...] = jnp.zeros_like(hid)

    def use(mm):
        wm = weights(mm)

        @pl.loop(0, nd)
        def _(t):
            hid[t] += jnp.dot(act[mm, t], wm, preferred_element_type=F32)

        flip[pl.ds(pl.multiple_of(mm * feat, feat), feat), :] = (
            act[mm].reshape(nd * tok, feat).T.astype(flip.dtype)
        )

    for a in range(1, nz + 1):
        zt = zo(a % nz)
        mm = zt * ny + y
        for b in range(1, ny):
            rcopy(part.at[mm], ry.at[a - 1, b - 1], py_s.at[a - 1, b], py_r.at[a - 1, b], mpeer(z, yo(b))).wait_recv()

        @pl.loop(0, nd)
        def _(t):
            total = part[mm, t].astype(F32)
            for b in range(1, ny):
                total += ry[a - 1, b - 1, t].astype(F32)
            part[mm, t] = total.astype(BF16)

        if a < nz:
            c = rcopy(part.at[mm], rz.at[a - 1], pz_s.at[a], pz_r.at[a], mpeer(zt, y))
            c.start()
            sends.append(c)
        use(zo(-(a % nz)) * ny + y)

    for s in range(nz):
        for b in range(1, ny):
            chunk = zo(-s) * ny + yo(-b)
            rcopy(act.at[chunk], act.at[chunk], ay_s.at[s, b], ay_r.at[s, b], mpeer(z, yo(b))).wait_recv()
            use(chunk)

    @pl.loop(0, nd)
    def _(t):
        hsend[t] = hid[t].astype(BF16)

    hid_sent = []
    for o in range(1, nd):
        c = rcopy(hsend.at[lax.rem(d + o, nd)], hrecv.at[o - 1], hd_s.at[o], hd_r.at[o], dpeer(o))
        c.start()
        hid_sent.append(c)

    for a in range(1, nz):
        rcopy(part.at[m], rz.at[a - 1], pz_s.at[a], pz_r.at[a], mpeer(zo(a), y)).wait_recv()

    @pl.loop(0, nd)
    def _(t):
        total = part[m, t].astype(F32)
        for a in range(1, nz):
            total += rz[a - 1, t].astype(F32)
        tot[t] = total.astype(BF16)

    ga_sent = []
    for o in range(1, nd):
        c = rcopy(tot.at[lax.rem(d + o, nd)], garecv.at[d], ga_s.at[o], ga_r.at[o], dpeer(o))
        c.start()
        ga_sent.append(c)
    garecv[d] = tot[d]

    for c in hid_sent:
        c.wait_recv()
    total = hid[d]
    for o in range(1, nd):
        total += hrecv[o - 1].astype(F32)
    hid_out[...] = total.astype(BF16)

    for c in ga_sent:
        c.wait_recv()
    for q in range(n_group):
        total = jnp.zeros((tok, group * blk), F32)
        for dd in range(nd):
            pick = select(group * blk, gw, width, dd * width)
            total += lax.dot_general(
                garecv[dd, :, q * gw:(q + 1) * gw], pick, (((1,), (1,)), ((), ())),
                preferred_element_type=F32,
            )
        ga_out[:, q * group * blk:(q + 1) * group * blk] = total.astype(BF16)

    for c in acts_sent + gout_sent + sends + hid_sent + ga_sent:
        c.wait_send()


def densify(rows_ref, count_ref, val_ref, w_ref):
    c = pl.program_id(0)
    slots, width = val_ref.shape[1:3]
    w_ref[...] = jnp.zeros_like(w_ref)

    @pl.loop(0, slots)
    def _(k):
        @pl.when(k < count_ref[c])
        def _():
            start = pl.multiple_of(rows_ref[c, k] * width, width)
            w_ref[pl.ds(start, width), :] = val_ref[0, k]


def weight_grad(rows_ref, count_ref, flip_ref, gout_ref, gv_ref, picked):
    c = pl.program_id(0)
    nd, tok, blk = gout_ref.shape
    slots, width = gv_ref.shape[1:3]

    for k in range(slots):
        live = k < count_ref[c]
        start = pl.multiple_of(jnp.where(live, rows_ref[c, k], 0) * width, width)
        picked[k * width:(k + 1) * width, :] = flip_ref[pl.ds(start, width), :]
    got = jnp.dot(
        picked[...].astype(BF16), gout_ref[...].reshape(nd * tok, blk), preferred_element_type=F32
    ).reshape(slots, width, blk)
    slot = lax.broadcasted_iota(jnp.int32, got.shape, 0)
    gv_ref[0] = jnp.where(slot < count_ref[c], got, 0.0)


def shards(nd, nm, acts, grad_out, values, block_rows, block_count):
    tok, local = acts.shape
    ff = grad_out.shape[1]
    cols, slots, width, blk = values.shape
    nz = N_Z
    ny = nm // nz
    local_blocks = local // blk
    feat = local_blocks * width
    depth = feat * nm
    if width % 16:
        values = values.astype(F32)
    dma = pltpu.SemaphoreType.DMA
    vmem = pl.BlockSpec(memory_space=pltpu.VMEM)
    smem = pl.BlockSpec(memory_space=pltpu.SMEM)
    limit = 62 * 2 ** 20
    dense = pl.pallas_call(
        densify,
        grid=(cols,),
        out_shape=jax.ShapeDtypeStruct((depth, ff), values.dtype),
        in_specs=[smem, smem, pl.BlockSpec((1, slots, width, blk), lambda c: (c, 0, 0, 0))],
        out_specs=pl.BlockSpec((depth, blk), lambda c: (0, c)),
        compiler_params=pltpu.CompilerParams(vmem_limit_bytes=limit),
    )(block_rows, block_count, values)
    hidden_out, grad_acts, flip, gall = pl.pallas_call(
        functools.partial(kernel, nd, nm),
        out_shape=(
            jax.ShapeDtypeStruct((tok, ff), BF16),
            jax.ShapeDtypeStruct((tok, local), BF16),
            jax.ShapeDtypeStruct((depth, nd * tok), values.dtype),
            jax.ShapeDtypeStruct((nd, tok, ff), BF16),
        ),
        in_specs=[vmem] * 3,
        out_specs=(vmem,) * 4,
        scratch_shapes=[
            pltpu.VMEM((nd, tok, feat), BF16),
            pltpu.VMEM((nm, nd, tok, feat), BF16),
            pltpu.VMEM((nm, nd, tok, feat), BF16),
            pltpu.VMEM((nz, ny - 1, nd, tok, feat), BF16),
            pltpu.VMEM((nz - 1, nd, tok, feat), BF16),
            pltpu.VMEM((nd, tok, ff), F32),
            pltpu.VMEM((nd, tok, ff), BF16),
            pltpu.VMEM((nd - 1, tok, ff), BF16),
            pltpu.VMEM((nd, tok, feat), BF16),
            pltpu.VMEM((nd, tok, feat), BF16),
            dma((nd,)), dma((nd,)), dma((nd,)), dma((nd,)),
            dma((nz,)), dma((nz,)), dma((nz, ny)), dma((nz, ny)),
            dma((nz, ny)), dma((nz, ny)), dma((nz,)), dma((nz,)),
            dma((nd,)), dma((nd,)), dma((nd,)), dma((nd,)),
        ],
        compiler_params=pltpu.CompilerParams(
            collective_id=0, has_side_effects=True, vmem_limit_bytes=limit
        ),
        cost_estimate=pl.CostEstimate(
            flops=4 * nd * tok * depth * ff, bytes_accessed=2 ** 23, transcendentals=0
        ),
    )(acts, grad_out, dense)
    grad_values = pl.pallas_call(
        weight_grad,
        grid=(cols,),
        out_shape=jax.ShapeDtypeStruct(values.shape, F32),
        in_specs=[
            smem, smem,
            pl.BlockSpec((depth, nd * tok), lambda c: (0, 0)),
            pl.BlockSpec((nd, tok, blk), lambda c: (0, 0, c)),
        ],
        out_specs=pl.BlockSpec((1, slots, width, blk), lambda c: (c, 0, 0, 0)),
        scratch_shapes=[pltpu.VMEM((slots * width, nd * tok), values.dtype)],
        compiler_params=pltpu.CompilerParams(vmem_limit_bytes=limit),
    )(block_rows, block_count, flip, gall)
    return hidden_out, grad_acts, grad_values


def solution(mesh):
    placed = (P("dp", "mp"), P("dp", "mp"), P("mp", None, "dp", None), P("mp", None), P("mp"))
    return jax.shard_map(
        functools.partial(shards, mesh.shape["dp"], mesh.shape["mp"]),
        mesh=mesh,
        in_specs=placed,
        out_specs=(P("dp", "mp"), P("dp", "mp"), P("mp", None, "dp", None)),
        check_vma=False,
    )
```

```python
import functools

import jax
import jax.numpy as jnp
from jax import lax
from jax.experimental import pallas as pl
from jax.experimental.pallas import tpu as pltpu
from jax.sharding import PartitionSpec as P

MESH = pl.DeviceIdType.MESH
BF16 = jnp.bfloat16
F32 = jnp.float32
N_Z = 4


def select(rows_in, lanes, width, shift):
    src = lax.broadcasted_iota(jnp.int32, (rows_in, lanes), 0)
    dst = lax.broadcasted_iota(jnp.int32, (rows_in, lanes), 1)
    hit = src == (dst // width) * 128 + shift + dst % width
    return jnp.where(hit, 1.0, 0.0).astype(BF16)


def kernel(
    nd, nm,
    rows_ref, slot_ref, acts_ref, gout_ref, val_hbm,
    hid_out, ga_out, gv_out,
    val, w, flip, gall, picked,
    perm, act, part, ry, rz, hid, hsend, hrecv, tot, gasend, garecv,
    val_s, aa_s, aa_r, go_s, go_r, gf_s, gf_r, az_s, az_r, ay_s, ay_r,
    py_s, py_r, pz_s, pz_r, hd_s, hd_r, ga_s, ga_r,
):
    nz = N_Z
    ny = nm // nz
    half = nd // 2
    d = lax.axis_index("dp")
    m = lax.axis_index("mp")
    z = m // ny
    y = m % ny
    h = d // 2
    core = d % 2
    twin = (h * 2 + 1 - core, m)
    tok, local = acts_ref.shape
    ff = gout_ref.shape[1]
    cols, slots, width, blk = val_hbm.shape
    feat = act.shape[3]
    local_blocks = local // blk
    group = min(local_blocks, blk // width)
    gw = group * width
    n_group = local_blocks // group
    row_blocks = local_blocks * nm

    def dpeer(o):
        return (lax.rem(d + o, nd), m)

    def hpeer(o):
        return (lax.rem(h + o, half) * 2 + core, m)

    def mpeer(zz, yy):
        return (d, zz * ny + yy)

    def yo(o):
        return lax.rem(y + o + ny, ny)

    def rcopy(src, dst, ss, rs, dev):
        return pltpu.make_async_remote_copy(
            src_ref=src, dst_ref=dst, send_sem=ss, recv_sem=rs, device_id=dev, device_id_type=MESH
        )

    load = pltpu.make_async_copy(val_hbm, val.at[:, 0:slots], val_s)
    load.start()

    barrier = pltpu.get_barrier_semaphore()
    peers = [dpeer(o) for o in range(1, nd)]
    peers += [mpeer(z, yo(b)) for b in range(1, ny)]

    def greet(peer):
        pl.semaphore_signal(barrier, inc=1, device_id=peer, device_id_type=MESH)

    for peer in peers:
        greet(peer)

    @pl.when(z > 0)
    def _():
        greet(mpeer(z - 1, y))

    @pl.when(z < nz - 1)
    def _():
        greet(mpeer(z + 1, y))

    for dd in range(nd):
        pick = select(group * blk, gw, width, dd * width)
        for q in range(n_group):
            got = jnp.dot(
                acts_ref[:, q * group * blk:(q + 1) * group * blk], pick, preferred_element_type=F32
            )
            perm[dd, :, q * gw:(q + 1) * gw] = got.astype(BF16)

    ends = (z == 0).astype(jnp.int32) + (z == nz - 1).astype(jnp.int32)
    pl.semaphore_wait(barrier, len(peers) + 2 - ends)

    sends = []

    def go(c):
        c.start()
        sends.append(c)
        return c

    acts_sent = [
        go(rcopy(perm.at[lax.rem(d + o, nd)], act.at[m, d], aa_s.at[o], aa_r.at[o], dpeer(o)))
        for o in range(1, nd)
    ]
    gout_sent = [
        go(rcopy(gout_ref, gall.at[d], go_s.at[o], go_r.at[o], hpeer(o))) for o in range(1, half)
    ]
    gout_twin = [go(rcopy(gout_ref, gall.at[d], gf_s.at[0], gf_r.at[0], twin))]
    act[m, d] = perm[d]
    gall[d] = gout_ref[...]

    load.wait()
    for c in range(cols):
        val[c, slots] = jnp.zeros((width, blk), val.dtype)

    @pl.loop(0, row_blocks, unroll=2)
    def _(r):
        for c in range(cols):
            w[pl.ds(pl.multiple_of(r * width, width), width), c * blk:(c + 1) * blk] = val[
                c, slot_ref[c, r]
            ]

    for c in acts_sent:
        c.wait_recv()

    def along(right, src):
        ref = act.at[src * ny + y]
        side = 0 if right else 1
        return rcopy(ref, ref, az_s.at[side, src], az_r.at[side, src], mpeer(z + 1 if right else z - 1, y))

    def across(src, b, back):
        ref = act.at[src * ny + (yo(-b) if back else y)]
        return rcopy(ref, ref, ay_s.at[src, b], ay_r.at[src, b], mpeer(z, yo(b)))

    def spread(src):
        for b in range(1, ny):
            across(src, b, False).start()

    @pl.when(z < nz - 1)
    def _():
        along(True, z).start()

    @pl.when(z > 0)
    def _():
        along(False, z).start()

    spread(z)

    def arrival(s):
        @pl.when(z >= s)
        def _():
            along(True, z - s).wait_recv()

            @pl.when(z < nz - 1)
            def _():
                along(True, z - s).start()

            spread(z - s)

        @pl.when(z + s < nz)
        def _():
            along(False, z + s).wait_recv()

            @pl.when(z > 0)
            def _():
                along(False, z + s).start()

            spread(z + s)

    for o, c in enumerate(gout_sent):
        c.wait_recv()
        ref = gall.at[lax.rem(h - (o + 1) + half, half) * 2 + core]
        gout_twin.append(go(rcopy(ref, ref, gf_s.at[o + 1], gf_r.at[o + 1], twin)))
    for c in gout_twin:
        c.wait_recv()

    def weights(mm):
        return w[pl.ds(pl.multiple_of(mm * feat, feat), feat), :].astype(BF16)

    def partial(mm):
        part[mm] = lax.dot_general(
            gall[...].reshape(nd * tok, ff), weights(mm), (((1,), (1,)), ((), ())),
            preferred_element_type=F32,
        ).astype(BF16).reshape(nd, tok, feat)

    def target(a):
        down = nz - 1 - a
        low = down - (down <= z).astype(jnp.int32)
        high = a + (jnp.int32(a) >= z).astype(jnp.int32)
        return z if a == nz - 1 else jnp.where(z < nz // 2, low, high)

    def to_y(a, b):
        return rcopy(
            part.at[target(a) * ny + yo(b)], ry.at[a, b - 1], py_s.at[a, b], py_r.at[a, b], mpeer(z, yo(b))
        )

    for a in range(nz):
        for b in range(1, ny):
            partial(target(a) * ny + yo(b))
            go(to_y(a, b))
        if a < nz - 1:
            arrival(a + 1)

    @pl.loop(0, nz)
    def _(zz):
        partial(zz * ny + y)

    hid[...] = jnp.zeros_like(hid)

    def use(mm):
        am = act[mm].reshape(nd * tok, feat)
        for lo in range(0, ff, 256):
            hi = min(lo + 256, ff)
            wm = w[pl.ds(pl.multiple_of(mm * feat, feat), feat), lo:hi].astype(BF16)
            hid[:, :, lo:hi] += jnp.dot(am, wm, preferred_element_type=F32).reshape(nd, tok, hi - lo)
        flip[pl.ds(mm * local_blocks, local_blocks)] = am.T.astype(flip.dtype).reshape(
            local_blocks, width, nd * tok
        )

    def sum_y(a):
        mm = target(a) * ny + y
        for b in range(1, ny):
            to_y(a, b).wait_recv()

        @pl.loop(0, nd)
        def _(t):
            total = part[mm, t].astype(F32)
            for b in range(1, ny):
                total += ry[a, b - 1, t].astype(F32)
            part[mm, t] = total.astype(BF16)

    def to_z(zt):
        right = (zt > z).astype(jnp.int32)
        return rcopy(
            part.at[zt * ny + y], rz.at[1 - right, zt], pz_s.at[1 - right, zt], pz_r.at[1 - right, zt],
            mpeer(z + 2 * right - 1, y),
        )

    def from_z(side, zt):
        ref = rz.at[side, zt]
        rcopy(ref, ref, pz_s.at[side, zt], pz_r.at[side, zt], mpeer(z, y)).wait_recv()

    def sum_z(a):
        zt = target(a)
        side = 1 - (zt > z).astype(jnp.int32)
        sum_y(a)

        @pl.when(jnp.where(zt > z, z > 0, z < nz - 1))
        def _():
            from_z(side, zt)

            @pl.loop(0, nd)
            def _(t):
                part[zt * ny + y, t] = (
                    part[zt * ny + y, t].astype(F32) + rz[side, zt, t].astype(F32)
                ).astype(BF16)

        to_z(zt).start()

    def use_far(s):
        src = lax.rem(z + s, nz)
        for b in range(1, ny):
            across(src, b, True).wait_recv()
            use(src * ny + yo(-b))

    sum_z(0)

    @pl.loop(0, nz)
    def _(zz):
        use(zz * ny + y)

    sum_z(1)

    @pl.loop(0, nz)
    def _(s):
        use_far(s)

    @pl.loop(0, nd)
    def _(t):
        hsend[t] = hid[t].astype(BF16)

    hid_sent = [
        go(rcopy(hsend.at[lax.rem(d + o, nd)], hrecv.at[o - 1], hd_s.at[o], hd_r.at[o], dpeer(o)))
        for o in range(1, nd)
    ]
    for a in range(2, nz - 1):
        sum_z(a)
    sum_y(nz - 1)

    for c in range(cols):
        for k in range(slots):
            picked[k * width:(k + 1) * width, :] = flip[rows_ref[c, k]]
        gv_out[c] = jnp.dot(
            picked[...].astype(BF16), gall[:, :, c * blk:(c + 1) * blk].reshape(nd * tok, blk),
            preferred_element_type=F32,
        ).reshape(slots, width, blk)

    @pl.loop(0, nd)
    def _(t):
        tot[t] = part[m, t].astype(F32)

    for side in range(2):
        @pl.when(z > 0 if side == 0 else z < nz - 1)
        def _():
            from_z(side, z)

            @pl.loop(0, nd)
            def _(t):
                tot[t] += rz[side, z, t].astype(F32)

    @pl.loop(0, nd)
    def _(t):
        gasend[t] = tot[t].astype(BF16)

    garecv[d] = gasend[d]

    ga_sent = [
        go(rcopy(gasend.at[lax.rem(d + o, nd)], garecv.at[d], ga_s.at[o], ga_r.at[o], dpeer(o)))
        for o in range(1, nd)
    ]

    for c in hid_sent:
        c.wait_recv()
    total = hid[d]
    for o in range(1, nd):
        total += hrecv[o - 1].astype(F32)
    hid_out[...] = total.astype(BF16)

    for c in ga_sent:
        c.wait_recv()
    for q in range(n_group):
        total = jnp.zeros((tok, group * blk), F32)
        for dd in range(nd):
            pick = select(group * blk, gw, width, dd * width)
            total += lax.dot_general(
                garecv[dd, :, q * gw:(q + 1) * gw], pick, (((1,), (1,)), ((), ())),
                preferred_element_type=F32,
            )
        ga_out[:, q * group * blk:(q + 1) * group * blk] = total.astype(BF16)

    for c in sends:
        c.wait_send()
    for src in range(nz):
        for b in range(1, ny):
            across(src, b, False).wait_send()

        @pl.when((z < nz - 1) & (z >= src))
        def _():
            along(True, src).wait_send()

        @pl.when((z > 0) & (z <= src))
        def _():
            along(False, src).wait_send()
    for a in range(nz - 1):
        to_z(target(a)).wait_send()


def shards(nd, nm, acts, grad_out, values, block_rows, block_count):
    tok, local = acts.shape
    ff = grad_out.shape[1]
    cols, slots, width, blk = values.shape
    nz = N_Z
    ny = nm // nz
    local_blocks = local // blk
    feat = local_blocks * width
    row_blocks = local_blocks * nm
    depth = feat * nm
    live = jnp.arange(slots, dtype=jnp.int32)[None, :] < block_count[:, None]
    hit = (block_rows[:, :, None] == jnp.arange(row_blocks, dtype=jnp.int32)) & live[:, :, None]
    slot_of = jnp.min(
        jnp.where(hit, jnp.arange(slots, dtype=jnp.int32)[None, :, None], slots), axis=1
    )
    if width % 16:
        values = values.astype(F32)
    kind = values.dtype
    dma = pltpu.SemaphoreType.DMA
    vmem = pl.BlockSpec(memory_space=pltpu.VMEM)
    smem = pl.BlockSpec(memory_space=pltpu.SMEM)
    hidden_out, grad_acts, grad_values = pl.pallas_call(
        functools.partial(kernel, nd, nm),
        out_shape=(
            jax.ShapeDtypeStruct((tok, ff), BF16),
            jax.ShapeDtypeStruct((tok, local), BF16),
            jax.ShapeDtypeStruct(values.shape, F32),
        ),
        in_specs=[smem] * 2 + [vmem] * 2 + [pl.BlockSpec(memory_space=pl.ANY)],
        out_specs=(vmem,) * 3,
        scratch_shapes=[
            pltpu.VMEM((cols, slots + 1, width, blk), kind),
            pltpu.VMEM((depth, ff), kind),
            pltpu.VMEM((row_blocks, width, nd * tok), kind),
            pltpu.VMEM((nd, tok, ff), BF16),
            pltpu.VMEM((slots * width, nd * tok), kind),
            pltpu.VMEM((nd, tok, feat), BF16),
            pltpu.VMEM((nm, nd, tok, feat), BF16),
            pltpu.VMEM((nm, nd, tok, feat), BF16),
            pltpu.VMEM((nz, ny - 1, nd, tok, feat), BF16),
            pltpu.VMEM((2, nz, nd, tok, feat), BF16),
            pltpu.VMEM((nd, tok, ff), F32),
            pltpu.VMEM((nd, tok, ff), BF16),
            pltpu.VMEM((nd - 1, tok, ff), BF16),
            pltpu.VMEM((nd, tok, feat), F32),
            pltpu.VMEM((nd, tok, feat), BF16),
            pltpu.VMEM((nd, tok, feat), BF16),
            dma(()),
            dma((nd,)), dma((nd,)), dma((nd,)), dma((nd,)), dma((nd,)), dma((nd,)),
            dma((2, nz)), dma((2, nz)), dma((nz, ny)), dma((nz, ny)),
            dma((nz, ny)), dma((nz, ny)), dma((2, nz)), dma((2, nz)),
            dma((nd,)), dma((nd,)), dma((nd,)), dma((nd,)),
        ],
        compiler_params=pltpu.CompilerParams(
            collective_id=0, has_side_effects=True, vmem_limit_bytes=62 * 2 ** 20
        ),
        cost_estimate=pl.CostEstimate(
            flops=4 * nd * tok * depth * ff, bytes_accessed=2 ** 23, transcendentals=0
        ),
    )(block_rows, slot_of, acts, grad_out, values)
    grad_values = jnp.where(live[:, :, None, None], grad_values, jnp.zeros((), F32))
    return hidden_out, grad_acts, grad_values


def solution(mesh):
    placed = (P("dp", "mp"), P("dp", "mp"), P("mp", None, "dp", None), P("mp", None), P("mp"))
    return jax.shard_map(
        functools.partial(shards, mesh.shape["dp"], mesh.shape["mp"]),
        mesh=mesh,
        in_specs=placed,
        out_specs=(P("dp", "mp"), P("dp", "mp"), P("mp", None, "dp", None)),
        check_vma=False,
    )
```

```python
import functools

import jax
import jax.numpy as jnp
from jax import lax
from jax.experimental import pallas as pl
from jax.experimental.pallas import tpu as pltpu
from jax.sharding import PartitionSpec as P

MESH = pl.DeviceIdType.MESH
BF16 = jnp.bfloat16
F32 = jnp.float32
N_Z = 4


def select(rows_in, lanes, width, shift):
    src = lax.broadcasted_iota(jnp.int32, (rows_in, lanes), 0)
    dst = lax.broadcasted_iota(jnp.int32, (rows_in, lanes), 1)
    hit = src == (dst // width) * 128 + shift + dst % width
    return jnp.where(hit, 1.0, 0.0).astype(BF16)


def kernel(
    nd, nm,
    rows_ref, slot_ref, acts_ref, gout_ref, val_hbm,
    hid_out, ga_out, gv_hbm,
    val, w, flip, gall, picked, picks, gv,
    perm, act, part, ry, rz, hid, hsend, hrecv, tot, gasend, garecv,
    val_s, gv_s, aa_s, aa_r, go_s, go_r, gf_s, gf_r, az_s, az_r, ay_s, ay_r,
    py_s, py_r, pz_s, pz_r, hd_s, hd_r, ga_s, ga_r,
):
    nz = N_Z
    ny = nm // nz
    half = nd // 2
    d = lax.axis_index("dp")
    m = lax.axis_index("mp")
    z = m // ny
    y = m % ny
    h = d // 2
    core = d % 2
    twin = (h * 2 + 1 - core, m)
    tok, local = acts_ref.shape
    ff = gout_ref.shape[1]
    cols, slots, width, blk = val_hbm.shape
    feat = act.shape[3]
    local_blocks = local // blk
    group = min(local_blocks, blk // width)
    gw = group * width
    n_group = local_blocks // group
    row_blocks = local_blocks * nm

    def dpeer(o):
        return (lax.rem(d + o, nd), m)

    def hpeer(o):
        return (lax.rem(h + o, half) * 2 + core, m)

    def mpeer(zz, yy):
        return (d, zz * ny + yy)

    def yo(o):
        return lax.rem(y + o + ny, ny)

    def rcopy(src, dst, ss, rs, dev):
        return pltpu.make_async_remote_copy(
            src_ref=src, dst_ref=dst, send_sem=ss, recv_sem=rs, device_id=dev, device_id_type=MESH
        )

    load = pltpu.make_async_copy(val_hbm, val.at[:, 0:slots], val_s)
    load.start()

    barrier = pltpu.get_barrier_semaphore()
    peers = [dpeer(o) for o in range(1, nd)]
    peers += [mpeer(z, yo(b)) for b in range(1, ny)]

    def greet(peer):
        pl.semaphore_signal(barrier, inc=1, device_id=peer, device_id_type=MESH)

    for peer in peers:
        greet(peer)

    @pl.when(z > 0)
    def _():
        greet(mpeer(z - 1, y))

    @pl.when(z < nz - 1)
    def _():
        greet(mpeer(z + 1, y))

    for dd in range(nd):
        picks[dd] = select(group * blk, gw, width, dd * width)
        for q in range(n_group):
            got = jnp.dot(
                acts_ref[:, q * group * blk:(q + 1) * group * blk], picks[dd], preferred_element_type=F32
            )
            perm[dd, :, q * gw:(q + 1) * gw] = got.astype(BF16)

    ends = (z == 0).astype(jnp.int32) + (z == nz - 1).astype(jnp.int32)
    pl.semaphore_wait(barrier, len(peers) + 2 - ends)

    sends = []

    def go(c):
        c.start()
        sends.append(c)
        return c

    acts_sent = [
        go(rcopy(perm.at[lax.rem(d + o, nd)], act.at[m, d], aa_s.at[o], aa_r.at[o], dpeer(o)))
        for o in range(1, nd)
    ]
    act[m, d] = perm[d]

    for c in acts_sent:
        c.wait_recv()

    def along(right, src):
        ref = act.at[src * ny + y]
        side = 0 if right else 1
        return rcopy(ref, ref, az_s.at[side, src], az_r.at[side, src], mpeer(z + 1 if right else z - 1, y))

    def across(src, b, back):
        ref = act.at[src * ny + (yo(-b) if back else y)]
        return rcopy(ref, ref, ay_s.at[src, b], ay_r.at[src, b], mpeer(z, yo(b)))

    def spread(src):
        for b in range(1, ny):
            across(src, b, False).start()

    @pl.when(z < nz - 1)
    def _():
        along(True, z).start()

    @pl.when(z > 0)
    def _():
        along(False, z).start()

    spread(z)

    def arrival(s):
        @pl.when(z >= s)
        def _():
            along(True, z - s).wait_recv()

            @pl.when(z < nz - 1)
            def _():
                along(True, z - s).start()

            spread(z - s)

        @pl.when(z + s < nz)
        def _():
            along(False, z + s).wait_recv()

            @pl.when(z > 0)
            def _():
                along(False, z + s).start()

            spread(z + s)

    gout_sent = [
        go(rcopy(gout_ref, gall.at[d], go_s.at[o], go_r.at[o], hpeer(o))) for o in range(1, half)
    ]
    gout_twin = [go(rcopy(gout_ref, gall.at[d], gf_s.at[0], gf_r.at[0], twin))]
    gall[d] = gout_ref[...]

    load.wait()
    for c in range(cols):
        val[c, slots] = jnp.zeros((width, blk), val.dtype)

    @pl.loop(0, row_blocks, unroll=2)
    def _(r):
        for c in range(cols):
            w[pl.ds(pl.multiple_of(r * width, width), width), c * blk:(c + 1) * blk] = val[
                c, slot_ref[c, r]
            ]

    for o, c in enumerate(gout_sent):
        c.wait_recv()
        ref = gall.at[lax.rem(h - (o + 1) + half, half) * 2 + core]
        gout_twin.append(go(rcopy(ref, ref, gf_s.at[o + 1], gf_r.at[o + 1], twin)))
    for c in gout_twin:
        c.wait_recv()

    def weights(mm):
        return w[pl.ds(pl.multiple_of(mm * feat, feat), feat), :].astype(BF16)

    def partial(mm):
        part[mm] = lax.dot_general(
            gall[...].reshape(nd * tok, ff), weights(mm), (((1,), (1,)), ((), ())),
            preferred_element_type=F32,
        ).astype(BF16).reshape(nd, tok, feat)

    def target(a):
        down = nz - 1 - a
        low = down - (down <= z).astype(jnp.int32)
        high = a + (jnp.int32(a) >= z).astype(jnp.int32)
        return z if a == nz - 1 else jnp.where(z < nz // 2, low, high)

    def to_y(a, b):
        return rcopy(
            part.at[target(a) * ny + yo(b)], ry.at[a, b - 1], py_s.at[a, b], py_r.at[a, b], mpeer(z, yo(b))
        )

    def send_y(a):
        for b in range(1, ny):
            go(to_y(a, b))

    for a in range(nz):
        for b in range(1, ny):
            partial(target(a) * ny + yo(b))
        if a < nz - 1:
            arrival(a + 1)
    send_y(0)

    @pl.loop(0, nz)
    def _(zz):
        partial(zz * ny + y)

    hid[...] = jnp.zeros_like(hid)

    def use(mm):
        am = act[mm].reshape(nd * tok, feat)
        for lo in range(0, ff, 256):
            hi = min(lo + 256, ff)
            wm = w[pl.ds(pl.multiple_of(mm * feat, feat), feat), lo:hi].astype(BF16)
            hid[:, :, lo:hi] += jnp.dot(am, wm, preferred_element_type=F32).reshape(nd, tok, hi - lo)
        flip[pl.ds(mm * local_blocks, local_blocks)] = am.T.astype(flip.dtype).reshape(
            local_blocks, width, nd * tok
        )

    def sum_y(a):
        mm = target(a) * ny + y
        for b in range(1, ny):
            to_y(a, b).wait_recv()

        @pl.loop(0, nd)
        def _(t):
            total = part[mm, t].astype(F32)
            for b in range(1, ny):
                total += ry[a, b - 1, t].astype(F32)
            part[mm, t] = total.astype(BF16)

    def to_z(zt):
        right = (zt > z).astype(jnp.int32)
        return rcopy(
            part.at[zt * ny + y], rz.at[1 - right, zt], pz_s.at[1 - right, zt], pz_r.at[1 - right, zt],
            mpeer(z + 2 * right - 1, y),
        )

    def from_z(side, zt):
        ref = rz.at[side, zt]
        rcopy(ref, ref, pz_s.at[side, zt], pz_r.at[side, zt], mpeer(z, y)).wait_recv()

    def sum_z(a):
        zt = target(a)
        side = 1 - (zt > z).astype(jnp.int32)
        sum_y(a)

        @pl.when(jnp.where(zt > z, z > 0, z < nz - 1))
        def _():
            from_z(side, zt)

            @pl.loop(0, nd)
            def _(t):
                part[zt * ny + y, t] = (
                    part[zt * ny + y, t].astype(F32) + rz[side, zt, t].astype(F32)
                ).astype(BF16)

        to_z(zt).start()

    def use_far(s):
        src = lax.rem(z + s, nz)
        for b in range(1, ny):
            across(src, b, True).wait_recv()
            use(src * ny + yo(-b))

    @pl.loop(0, nz)
    def _(zz):
        use(zz * ny + y)

    send_y(1)

    @pl.loop(0, nz)
    def _(s):
        use_far(s)

    @pl.loop(0, nd)
    def _(t):
        hsend[t] = hid[t].astype(BF16)

    hid_sent = [
        go(rcopy(hsend.at[lax.rem(d + o, nd)], hrecv.at[o - 1], hd_s.at[o], hd_r.at[o], dpeer(o)))
        for o in range(1, nd)
    ]

    saves = []

    def block_grad(c):
        for k in range(slots):
            picked[k * width:(k + 1) * width, :] = flip[rows_ref[c, k]]
        gv[c] = jnp.dot(
            picked[...].astype(BF16), gall[:, :, c * blk:(c + 1) * blk].reshape(nd * tok, blk),
            preferred_element_type=F32,
        ).reshape(slots, width, blk).astype(gv.dtype)
        saves.append(pltpu.make_async_copy(gv.at[c], gv_hbm.at[c], gv_s.at[c]))
        saves[-1].start()

    sum_z(0)
    for a in range(2, nz):
        send_y(a)
        for c in range(cols * (a - 2) // (nz - 2), cols * (a - 1) // (nz - 2)):
            block_grad(c)
        if a < nz - 1:
            sum_z(a - 1)
    for a in range(max(1, nz - 2), nz - 1):
        sum_z(a)
    sum_y(nz - 1)

    @pl.loop(0, nd)
    def _(t):
        tot[t] = part[m, t].astype(F32)

    for side in range(2):
        @pl.when(z > 0 if side == 0 else z < nz - 1)
        def _():
            from_z(side, z)

            @pl.loop(0, nd)
            def _(t):
                tot[t] += rz[side, z, t].astype(F32)

    @pl.loop(0, nd)
    def _(t):
        gasend[t] = tot[t].astype(BF16)

    garecv[d] = gasend[d]

    ga_sent = [
        go(rcopy(gasend.at[lax.rem(d + o, nd)], garecv.at[d], ga_s.at[o], ga_r.at[o], dpeer(o)))
        for o in range(1, nd)
    ]

    for c in hid_sent:
        c.wait_recv()
    total = hid[d]
    for o in range(1, nd):
        total += hrecv[o - 1].astype(F32)
    hid_out[...] = total.astype(BF16)

    for c in ga_sent:
        c.wait_recv()
    for q in range(n_group):
        total = jnp.zeros((tok, group * blk), F32)
        for dd in range(nd):
            total += lax.dot_general(
                garecv[dd, :, q * gw:(q + 1) * gw], picks[dd], (((1,), (1,)), ((), ())),
                preferred_element_type=F32,
            )
        ga_out[:, q * group * blk:(q + 1) * group * blk] = total.astype(BF16)

    for c in saves:
        c.wait()
    for c in sends:
        c.wait_send()
    for src in range(nz):
        for b in range(1, ny):
            across(src, b, False).wait_send()

        @pl.when((z < nz - 1) & (z >= src))
        def _():
            along(True, src).wait_send()

        @pl.when((z > 0) & (z <= src))
        def _():
            along(False, src).wait_send()
    for a in range(nz - 1):
        to_z(target(a)).wait_send()


def shards(nd, nm, acts, grad_out, values, block_rows, block_count):
    tok, local = acts.shape
    ff = grad_out.shape[1]
    cols, slots, width, blk = values.shape
    nz = N_Z
    ny = nm // nz
    local_blocks = local // blk
    feat = local_blocks * width
    row_blocks = local_blocks * nm
    depth = feat * nm
    group = min(local_blocks, blk // width)
    live = jnp.arange(slots, dtype=jnp.int32)[None, :] < block_count[:, None]
    hit = (block_rows[:, :, None] == jnp.arange(row_blocks, dtype=jnp.int32)) & live[:, :, None]
    slot_of = jnp.min(
        jnp.where(hit, jnp.arange(slots, dtype=jnp.int32)[None, :, None], slots), axis=1
    )
    if width % 16:
        values = values.astype(F32)
    kind = values.dtype
    dma = pltpu.SemaphoreType.DMA
    vmem = pl.BlockSpec(memory_space=pltpu.VMEM)
    smem = pl.BlockSpec(memory_space=pltpu.SMEM)
    hidden_out, grad_acts, grad_values = pl.pallas_call(
        functools.partial(kernel, nd, nm),
        out_shape=(
            jax.ShapeDtypeStruct((tok, ff), BF16),
            jax.ShapeDtypeStruct((tok, local), BF16),
            jax.ShapeDtypeStruct(values.shape, kind),
        ),
        in_specs=[smem] * 2 + [vmem] * 2 + [pl.BlockSpec(memory_space=pl.ANY)],
        out_specs=(vmem, vmem, pl.BlockSpec(memory_space=pl.ANY)),
        scratch_shapes=[
            pltpu.VMEM((cols, slots + 1, width, blk), kind),
            pltpu.VMEM((depth, ff), kind),
            pltpu.VMEM((row_blocks, width, nd * tok), kind),
            pltpu.VMEM((nd, tok, ff), BF16),
            pltpu.VMEM((slots * width, nd * tok), kind),
            pltpu.VMEM((nd, group * blk, group * width), BF16),
            pltpu.VMEM(values.shape, kind),
            pltpu.VMEM((nd, tok, feat), BF16),
            pltpu.VMEM((nm, nd, tok, feat), BF16),
            pltpu.VMEM((nm, nd, tok, feat), BF16),
            pltpu.VMEM((nz, ny - 1, nd, tok, feat), BF16),
            pltpu.VMEM((2, nz, nd, tok, feat), BF16),
            pltpu.VMEM((nd, tok, ff), F32),
            pltpu.VMEM((nd, tok, ff), BF16),
            pltpu.VMEM((nd - 1, tok, ff), BF16),
            pltpu.VMEM((nd, tok, feat), F32),
            pltpu.VMEM((nd, tok, feat), BF16),
            pltpu.VMEM((nd, tok, feat), BF16),
            dma(()), dma((cols,)),
            dma((nd,)), dma((nd,)), dma((nd,)), dma((nd,)), dma((nd,)), dma((nd,)),
            dma((2, nz)), dma((2, nz)), dma((nz, ny)), dma((nz, ny)),
            dma((nz, ny)), dma((nz, ny)), dma((2, nz)), dma((2, nz)),
            dma((nd,)), dma((nd,)), dma((nd,)), dma((nd,)),
        ],
        compiler_params=pltpu.CompilerParams(
            collective_id=0, has_side_effects=True, vmem_limit_bytes=62 * 2 ** 20
        ),
        cost_estimate=pl.CostEstimate(
            flops=4 * nd * tok * depth * ff, bytes_accessed=2 ** 23, transcendentals=0
        ),
    )(block_rows, slot_of, acts, grad_out, values)
    grad_values = jnp.where(live[:, :, None, None], grad_values.astype(F32), jnp.zeros((), F32))
    return hidden_out, grad_acts, grad_values


def solution(mesh):
    placed = (P("dp", "mp"), P("dp", "mp"), P("mp", None, "dp", None), P("mp", None), P("mp"))
    return jax.shard_map(
        functools.partial(shards, mesh.shape["dp"], mesh.shape["mp"]),
        mesh=mesh,
        in_specs=placed,
        out_specs=(P("dp", "mp"), P("dp", "mp"), P("mp", None, "dp", None)),
        check_vma=False,
    )
```

```python
import functools

import jax
import jax.numpy as jnp
from jax import lax
from jax.experimental import pallas as pl
from jax.experimental.pallas import tpu as pltpu
from jax.sharding import PartitionSpec as P

MESH = pl.DeviceIdType.MESH
BF16 = jnp.bfloat16
F32 = jnp.float32
N_Z = 4


def select(rows_in, lanes, width, shift):
    src = lax.broadcasted_iota(jnp.int32, (rows_in, lanes), 0)
    dst = lax.broadcasted_iota(jnp.int32, (rows_in, lanes), 1)
    hit = src == (dst // width) * 128 + shift + dst % width
    return jnp.where(hit, 1.0, 0.0).astype(BF16)


def kernel(
    nd, nm,
    rows_ref, slot_ref, acts_ref, gout_ref, val_hbm,
    hid_out, ga_out, gv_hbm,
    val, w, flip, gall, picked, picks, gv,
    perm, act, part, ry, rz, hid, hsend, hrecv, tot, gasend, garecv,
    val_s, gv_s, aa_s, aa_r, go_s, go_r, gf_s, gf_r, az_s, az_r, ay_s, ay_r,
    py_s, py_r, pz_s, pz_r, hd_s, hd_r, ga_s, ga_r,
):
    nz = N_Z
    ny = nm // nz
    half = nd // 2
    d = lax.axis_index("dp")
    m = lax.axis_index("mp")
    z = m // ny
    y = m % ny
    h = d // 2
    core = d % 2
    twin = (h * 2 + 1 - core, m)
    tok, local = acts_ref.shape
    ff = gout_ref.shape[1]
    cols, slots, width, blk = val_hbm.shape
    feat = act.shape[3]
    local_blocks = local // blk
    group = min(local_blocks, blk // width)
    gw = group * width
    n_group = local_blocks // group
    row_blocks = local_blocks * nm

    def dpeer(o):
        return (lax.rem(d + o, nd), m)

    def hpeer(o):
        return (lax.rem(h + o, half) * 2 + core, m)

    def mpeer(zz, yy):
        return (d, zz * ny + yy)

    def yo(o):
        return lax.rem(y + o + ny, ny)

    def rcopy(src, dst, ss, rs, dev):
        return pltpu.make_async_remote_copy(
            src_ref=src, dst_ref=dst, send_sem=ss, recv_sem=rs, device_id=dev, device_id_type=MESH
        )

    load = pltpu.make_async_copy(val_hbm, val.at[:, 0:slots], val_s)
    load.start()

    barrier = pltpu.get_barrier_semaphore()
    peers = [dpeer(o) for o in range(1, nd)]
    peers += [mpeer(z, yo(b)) for b in range(1, ny)]

    def greet(peer):
        pl.semaphore_signal(barrier, inc=1, device_id=peer, device_id_type=MESH)

    for peer in peers:
        greet(peer)

    @pl.when(z > 0)
    def _():
        greet(mpeer(z - 1, y))

    @pl.when(z < nz - 1)
    def _():
        greet(mpeer(z + 1, y))

    for dd in range(nd):
        picks[dd] = select(group * blk, gw, width, dd * width)
        for q in range(n_group):
            got = jnp.dot(
                acts_ref[:, q * group * blk:(q + 1) * group * blk], picks[dd], preferred_element_type=F32
            )
            perm[dd, :, q * gw:(q + 1) * gw] = got.astype(BF16)

    ends = (z == 0).astype(jnp.int32) + (z == nz - 1).astype(jnp.int32)
    pl.semaphore_wait(barrier, len(peers) + 2 - ends)

    sends = []

    def go(c):
        c.start()
        sends.append(c)
        return c

    acts_sent = [
        go(rcopy(perm.at[lax.rem(d + o, nd)], act.at[m, d], aa_s.at[o], aa_r.at[o], dpeer(o)))
        for o in range(1, nd)
    ]
    act[m, d] = perm[d]

    def along(right, src, t):
        ref = act.at[src * ny + y, t]
        side = 0 if right else 1
        dev = mpeer(z + 1 if right else z - 1, y)
        return rcopy(ref, ref, az_s.at[side, src, t], az_r.at[side, src, t], dev)

    def across(src, b, back, t):
        ref = act.at[src * ny + (yo(-b) if back else y), t]
        return rcopy(ref, ref, ay_s.at[src, b, t], ay_r.at[src, b, t], mpeer(z, yo(b)))

    def spread(src, t):
        for b in range(1, ny):
            across(src, b, False, t).start()

    for o in range(nd):
        if o:
            acts_sent[o - 1].wait_recv()
        block = lax.rem(d - o + nd, nd)

        @pl.when(z < nz - 1)
        def _():
            along(True, z, block).start()

        @pl.when(z > 0)
        def _():
            along(False, z, block).start()

        spread(z, block)

    def arrival(s):
        @pl.loop(0, nd)
        def _(o):
            t = lax.rem(d - o + nd, nd)

            @pl.when(z >= s)
            def _():
                along(True, z - s, t).wait_recv()

                @pl.when(z < nz - 1)
                def _():
                    along(True, z - s, t).start()

                spread(z - s, t)

            @pl.when(z + s < nz)
            def _():
                along(False, z + s, t).wait_recv()

                @pl.when(z > 0)
                def _():
                    along(False, z + s, t).start()

                spread(z + s, t)

    gout_sent = [
        go(rcopy(gout_ref, gall.at[d], go_s.at[o], go_r.at[o], hpeer(o))) for o in range(1, half)
    ]
    gout_twin = [go(rcopy(gout_ref, gall.at[d], gf_s.at[0], gf_r.at[0], twin))]
    gall[d] = gout_ref[...]

    load.wait()
    for c in range(cols):
        val[c, slots] = jnp.zeros((width, blk), val.dtype)

    @pl.loop(0, row_blocks, unroll=2)
    def _(r):
        for c in range(cols):
            w[pl.ds(pl.multiple_of(r * width, width), width), c * blk:(c + 1) * blk] = val[
                c, slot_ref[c, r]
            ]

    for o, c in enumerate(gout_sent):
        c.wait_recv()
        ref = gall.at[lax.rem(h - (o + 1) + half, half) * 2 + core]
        gout_twin.append(go(rcopy(ref, ref, gf_s.at[o + 1], gf_r.at[o + 1], twin)))
    for c in gout_twin:
        c.wait_recv()

    def weights(mm):
        return w[pl.ds(pl.multiple_of(mm * feat, feat), feat), :].astype(BF16)

    def partial(mm):
        part[mm] = lax.dot_general(
            gall[...].reshape(nd * tok, ff), weights(mm), (((1,), (1,)), ((), ())),
            preferred_element_type=F32,
        ).astype(BF16).reshape(nd, tok, feat)

    def target(a):
        down = nz - 1 - a
        low = down - (down <= z).astype(jnp.int32)
        high = a + (jnp.int32(a) >= z).astype(jnp.int32)
        return z if a == nz - 1 else jnp.where(z < nz // 2, low, high)

    def to_y(a, b, t):
        return rcopy(
            part.at[target(a) * ny + yo(b), t], ry.at[a, b - 1, t], py_s.at[a, b, t], py_r.at[a, b, t],
            mpeer(z, yo(b)),
        )

    for a in range(nz):
        for b in range(1, ny):
            partial(target(a) * ny + yo(b))

            @pl.loop(0, nd)
            def _(t):
                to_y(a, b, t).start()

        if a < nz - 1:
            arrival(a + 1)

    @pl.loop(0, nz)
    def _(zz):
        partial(zz * ny + y)

    hid[...] = jnp.zeros_like(hid)

    def use(mm):
        am = act[mm].reshape(nd * tok, feat)
        for lo in range(0, ff, 256):
            hi = min(lo + 256, ff)
            wm = w[pl.ds(pl.multiple_of(mm * feat, feat), feat), lo:hi].astype(BF16)
            hid[:, :, lo:hi] += jnp.dot(am, wm, preferred_element_type=F32).reshape(nd, tok, hi - lo)
        flip[pl.ds(mm * local_blocks, local_blocks)] = am.T.astype(flip.dtype).reshape(
            local_blocks, width, nd * tok
        )

    def to_z(zt, t):
        right = (zt > z).astype(jnp.int32)
        return rcopy(
            part.at[zt * ny + y, t], rz.at[1 - right, zt, t],
            pz_s.at[1 - right, zt, t], pz_r.at[1 - right, zt, t],
            mpeer(z + 2 * right - 1, y),
        )

    def from_z(side, zt, t):
        ref = rz.at[side, zt, t]
        rcopy(ref, ref, pz_s.at[side, zt, t], pz_r.at[side, zt, t], mpeer(z, y)).wait_recv()

    def over_y(a, t):
        total = part[target(a) * ny + y, t].astype(F32)
        for b in range(1, ny):
            to_y(a, b, t).wait_recv()
            total += ry[a, b - 1, t].astype(F32)
        return total

    def sum_z(a):
        zt = target(a)
        mm = zt * ny + y
        side = 1 - (zt > z).astype(jnp.int32)
        middle = jnp.where(zt > z, z > 0, z < nz - 1)

        @pl.loop(0, nd)
        def _(t):
            total = over_y(a, t)

            @pl.when(middle)
            def _():
                from_z(side, zt, t)
                part[mm, t] = (total + rz[side, zt, t].astype(F32)).astype(BF16)

            @pl.when(jnp.logical_not(middle))
            def _():
                part[mm, t] = total.astype(BF16)

            to_z(zt, t).start()

    def use_far(s):
        src = lax.rem(z + s, nz)
        for b in range(1, ny):
            @pl.loop(0, nd)
            def _(t):
                across(src, b, True, t).wait_recv()

            use(src * ny + yo(-b))

    sum_z(0)

    @pl.loop(0, nz)
    def _(zz):
        use(zz * ny + y)

    sum_z(1)

    @pl.loop(0, nz)
    def _(s):
        use_far(s)

    @pl.loop(0, nd)
    def _(t):
        hsend[t] = hid[t].astype(BF16)

    hid_sent = [
        go(rcopy(hsend.at[lax.rem(d + o, nd)], hrecv.at[o - 1], hd_s.at[o], hd_r.at[o], dpeer(o)))
        for o in range(1, nd)
    ]

    saves = []

    def block_grad(c):
        for k in range(slots):
            picked[k * width:(k + 1) * width, :] = flip[rows_ref[c, k]]
        gv[c] = jnp.dot(
            picked[...].astype(BF16), gall[:, :, c * blk:(c + 1) * blk].reshape(nd * tok, blk),
            preferred_element_type=F32,
        ).reshape(slots, width, blk).astype(gv.dtype)
        saves.append(pltpu.make_async_copy(gv.at[c], gv_hbm.at[c], gv_s.at[c]))
        saves[-1].start()

    for c in range(cols // 2):
        block_grad(c)
    for a in range(2, nz - 1):
        sum_z(a)

    def to_dp(t):
        return rcopy(gasend.at[t], garecv.at[d], ga_s.at[t], ga_r.at[d], (t, m))

    @pl.loop(0, nd)
    def _(o):
        t = lax.rem(d + 1 + o, nd)
        tot[...] = over_y(nz - 1, t)
        for side in range(2):
            @pl.when(z > 0 if side == 0 else z < nz - 1)
            def _():
                from_z(side, z, t)
                tot[...] += rz[side, z, t].astype(F32)
        gasend[t] = tot[...].astype(BF16)

        @pl.when(t != d)
        def _():
            to_dp(t).start()

    garecv[d] = gasend[d]
    for c in range(cols // 2, cols):
        block_grad(c)

    for c in hid_sent:
        c.wait_recv()
    total = hid[d]
    for o in range(1, nd):
        total += hrecv[o - 1].astype(F32)
    hid_out[...] = total.astype(BF16)

    for o in range(1, nd):
        src = lax.rem(d + o, nd)
        rcopy(gasend.at[src], garecv.at[src], ga_s.at[src], ga_r.at[src], (src, m)).wait_recv()
    for q in range(n_group):
        total = jnp.zeros((tok, group * blk), F32)
        for dd in range(nd):
            total += lax.dot_general(
                garecv[dd, :, q * gw:(q + 1) * gw], picks[dd], (((1,), (1,)), ((), ())),
                preferred_element_type=F32,
            )
        ga_out[:, q * group * blk:(q + 1) * group * blk] = total.astype(BF16)

    for c in saves:
        c.wait()
    for c in sends:
        c.wait_send()

    @pl.loop(0, nd)
    def _(t):
        for src in range(nz):
            for b in range(1, ny):
                across(src, b, False, t).wait_send()
                to_y(src, b, t).wait_send()

            @pl.when((z < nz - 1) & (z >= src))
            def _():
                along(True, src, t).wait_send()

            @pl.when((z > 0) & (z <= src))
            def _():
                along(False, src, t).wait_send()

        for a in range(nz - 1):
            to_z(target(a), t).wait_send()

        @pl.when(t != d)
        def _():
            to_dp(t).wait_send()


def shards(nd, nm, acts, grad_out, values, block_rows, block_count):
    tok, local = acts.shape
    ff = grad_out.shape[1]
    cols, slots, width, blk = values.shape
    nz = N_Z
    ny = nm // nz
    local_blocks = local // blk
    feat = local_blocks * width
    row_blocks = local_blocks * nm
    depth = feat * nm
    group = min(local_blocks, blk // width)
    live = jnp.arange(slots, dtype=jnp.int32)[None, :] < block_count[:, None]
    hit = (block_rows[:, :, None] == jnp.arange(row_blocks, dtype=jnp.int32)) & live[:, :, None]
    slot_of = jnp.min(
        jnp.where(hit, jnp.arange(slots, dtype=jnp.int32)[None, :, None], slots), axis=1
    )
    if width % 16:
        values = values.astype(F32)
    kind = values.dtype
    dma = pltpu.SemaphoreType.DMA
    vmem = pl.BlockSpec(memory_space=pltpu.VMEM)
    smem = pl.BlockSpec(memory_space=pltpu.SMEM)
    hidden_out, grad_acts, grad_values = pl.pallas_call(
        functools.partial(kernel, nd, nm),
        out_shape=(
            jax.ShapeDtypeStruct((tok, ff), BF16),
            jax.ShapeDtypeStruct((tok, local), BF16),
            jax.ShapeDtypeStruct(values.shape, kind),
        ),
        in_specs=[smem] * 2 + [vmem] * 2 + [pl.BlockSpec(memory_space=pl.ANY)],
        out_specs=(vmem, vmem, pl.BlockSpec(memory_space=pl.ANY)),
        scratch_shapes=[
            pltpu.VMEM((cols, slots + 1, width, blk), kind),
            pltpu.VMEM((depth, ff), kind),
            pltpu.VMEM((row_blocks, width, nd * tok), kind),
            pltpu.VMEM((nd, tok, ff), BF16),
            pltpu.VMEM((slots * width, nd * tok), kind),
            pltpu.VMEM((nd, group * blk, group * width), BF16),
            pltpu.VMEM(values.shape, kind),
            pltpu.VMEM((nd, tok, feat), BF16),
            pltpu.VMEM((nm, nd, tok, feat), BF16),
            pltpu.VMEM((nm, nd, tok, feat), BF16),
            pltpu.VMEM((nz, ny - 1, nd, tok, feat), BF16),
            pltpu.VMEM((2, nz, nd, tok, feat), BF16),
            pltpu.VMEM((nd, tok, ff), F32),
            pltpu.VMEM((nd, tok, ff), BF16),
            pltpu.VMEM((nd - 1, tok, ff), BF16),
            pltpu.VMEM((tok, feat), F32),
            pltpu.VMEM((nd, tok, feat), BF16),
            pltpu.VMEM((nd, tok, feat), BF16),
            dma(()), dma((cols,)),
            dma((nd,)), dma((nd,)), dma((nd,)), dma((nd,)), dma((nd,)), dma((nd,)),
            dma((2, nz, nd)), dma((2, nz, nd)), dma((nz, ny, nd)), dma((nz, ny, nd)),
            dma((nz, ny, nd)), dma((nz, ny, nd)), dma((2, nz, nd)), dma((2, nz, nd)),
            dma((nd,)), dma((nd,)), dma((nd,)), dma((nd,)),
        ],
        compiler_params=pltpu.CompilerParams(
            collective_id=0, has_side_effects=True, vmem_limit_bytes=62 * 2 ** 20
        ),
        cost_estimate=pl.CostEstimate(
            flops=4 * nd * tok * depth * ff, bytes_accessed=2 ** 23, transcendentals=0
        ),
    )(block_rows, slot_of, acts, grad_out, values)
    grad_values = jnp.where(live[:, :, None, None], grad_values.astype(F32), jnp.zeros((), F32))
    return hidden_out, grad_acts, grad_values


def solution(mesh):
    placed = (P("dp", "mp"), P("dp", "mp"), P("mp", None, "dp", None), P("mp", None), P("mp"))
    return jax.shard_map(
        functools.partial(shards, mesh.shape["dp"], mesh.shape["mp"]),
        mesh=mesh,
        in_specs=placed,
        out_specs=(P("dp", "mp"), P("dp", "mp"), P("mp", None, "dp", None)),
        check_vma=False,
    )
```

```python
import functools

import jax
import jax.numpy as jnp
from jax import lax
from jax.experimental import pallas as pl
from jax.experimental.pallas import tpu as pltpu
from jax.sharding import PartitionSpec as P

MESH = pl.DeviceIdType.MESH
BF16 = jnp.bfloat16
F32 = jnp.float32
N_Z = 4


def select(rows_in, lanes, width, shift):
    src = lax.broadcasted_iota(jnp.int32, (rows_in, lanes), 0)
    dst = lax.broadcasted_iota(jnp.int32, (rows_in, lanes), 1)
    hit = src == (dst // width) * 128 + shift + dst % width
    return jnp.where(hit, 1.0, 0.0).astype(BF16)


def kernel(
    nd, nm,
    rows_ref, count_ref, acts_ref, gout_ref, val_hbm,
    hid_out, ga_out, gv_hbm,
    slot_v, slot_ref, val, w, flip, gall, picked, picks, gv,
    perm, act, part, ry, rz, hid, hsend, hrecv, tot, gasend, garecv,
    val_s, slot_s, gv_s, aa_s, aa_r, go_s, go_r, gf_s, gf_r, az_s, az_r, ay_s, ay_r,
    py_s, py_r, pz_s, pz_r, hd_s, hd_r, ga_s, ga_r,
):
    nz = N_Z
    ny = nm // nz
    half = nd // 2
    d = lax.axis_index("dp")
    m = lax.axis_index("mp")
    z = m // ny
    y = m % ny
    h = d // 2
    core = d % 2
    twin = (h * 2 + 1 - core, m)
    tok, local = acts_ref.shape
    ff = gout_ref.shape[1]
    cols, slots, width, blk = val_hbm.shape
    feat = act.shape[3]
    local_blocks = local // blk
    group = min(local_blocks, blk // width)
    gw = group * width
    n_group = local_blocks // group
    row_blocks = local_blocks * nm

    def dpeer(o):
        return (lax.rem(d + o, nd), m)

    def hpeer(o):
        return (lax.rem(h + o, half) * 2 + core, m)

    def mpeer(zz, yy):
        return (d, zz * ny + yy)

    def yo(o):
        return lax.rem(y + o + ny, ny)

    def rcopy(src, dst, ss, rs, dev):
        return pltpu.make_async_remote_copy(
            src_ref=src, dst_ref=dst, send_sem=ss, recv_sem=rs, device_id=dev, device_id_type=MESH
        )

    load = pltpu.make_async_copy(val_hbm, val.at[:, 0:slots], val_s)
    load.start()

    barrier = pltpu.get_barrier_semaphore()
    peers = [dpeer(o) for o in range(1, nd)]
    peers += [mpeer(z, yo(b)) for b in range(1, ny)]

    def greet(peer):
        pl.semaphore_signal(barrier, inc=1, device_id=peer, device_id_type=MESH)

    for peer in peers:
        greet(peer)

    @pl.when(z > 0)
    def _():
        greet(mpeer(z - 1, y))

    @pl.when(z < nz - 1)
    def _():
        greet(mpeer(z + 1, y))

    for dd in range(nd):
        picks[dd] = select(group * blk, gw, width, dd * width)
        for q in range(n_group):
            got = jnp.dot(
                acts_ref[:, q * group * blk:(q + 1) * group * blk], picks[dd], preferred_element_type=F32
            )
            perm[dd, :, q * gw:(q + 1) * gw] = got.astype(BF16)

    lane = lax.broadcasted_iota(jnp.int32, (1, slot_v.shape[1]), 1)
    slot_v[...] = jnp.zeros_like(slot_v)
    for c in range(cols):
        found = jnp.full(lane.shape, slots, jnp.int32)
        for k in range(slots):
            row = jnp.where(k < count_ref[c], rows_ref[c, k], -1)
            found = jnp.where(lane == row, k, found)
        slot_v[c:c + 1, :] = found
    to_scalar = pltpu.make_async_copy(slot_v, slot_ref, slot_s)
    to_scalar.start()

    ends = (z == 0).astype(jnp.int32) + (z == nz - 1).astype(jnp.int32)
    pl.semaphore_wait(barrier, len(peers) + 2 - ends)

    sends = []

    def go(c):
        c.start()
        sends.append(c)
        return c

    acts_sent = [
        go(rcopy(perm.at[lax.rem(d + o, nd)], act.at[m, d], aa_s.at[o], aa_r.at[o], dpeer(o)))
        for o in range(1, nd)
    ]
    gout_sent = [
        go(rcopy(gout_ref, gall.at[d], go_s.at[o], go_r.at[o], hpeer(o))) for o in range(1, half)
    ]
    gout_twin = [go(rcopy(gout_ref, gall.at[d], gf_s.at[0], gf_r.at[0], twin))]
    act[m, d] = perm[d]
    gall[d] = gout_ref[...]

    load.wait()
    to_scalar.wait()
    for c in range(cols):
        val[c, slots] = jnp.zeros((width, blk), val.dtype)

    @pl.loop(0, row_blocks, unroll=2)
    def _(r):
        for c in range(cols):
            w[pl.ds(pl.multiple_of(r * width, width), width), c * blk:(c + 1) * blk] = val[
                c, slot_ref[c, r]
            ]

    for c in acts_sent:
        c.wait_recv()

    def along(right, src):
        ref = act.at[src * ny + y]
        side = 0 if right else 1
        return rcopy(ref, ref, az_s.at[side, src], az_r.at[side, src], mpeer(z + 1 if right else z - 1, y))

    def across(src, b, back):
        ref = act.at[src * ny + (yo(-b) if back else y)]
        return rcopy(ref, ref, ay_s.at[src, b], ay_r.at[src, b], mpeer(z, yo(b)))

    def spread(src):
        for b in range(1, ny):
            across(src, b, False).start()

    @pl.when(z < nz - 1)
    def _():
        along(True, z).start()

    @pl.when(z > 0)
    def _():
        along(False, z).start()

    spread(z)

    def arrival(s):
        @pl.when(z >= s)
        def _():
            along(True, z - s).wait_recv()

            @pl.when(z < nz - 1)
            def _():
                along(True, z - s).start()

            spread(z - s)

        @pl.when(z + s < nz)
        def _():
            along(False, z + s).wait_recv()

            @pl.when(z > 0)
            def _():
                along(False, z + s).start()

            spread(z + s)

    for o, c in enumerate(gout_sent):
        c.wait_recv()
        ref = gall.at[lax.rem(h - (o + 1) + half, half) * 2 + core]
        gout_twin.append(go(rcopy(ref, ref, gf_s.at[o + 1], gf_r.at[o + 1], twin)))
    for c in gout_twin:
        c.wait_recv()

    def weights(mm):
        return w[pl.ds(pl.multiple_of(mm * feat, feat), feat), :].astype(BF16)

    def partial(mm):
        part[mm] = lax.dot_general(
            gall[...].reshape(nd * tok, ff), weights(mm), (((1,), (1,)), ((), ())),
            preferred_element_type=F32,
        ).astype(BF16).reshape(nd, tok, feat)

    def target(a):
        down = nz - 1 - a
        low = down - (down <= z).astype(jnp.int32)
        high = a + (jnp.int32(a) >= z).astype(jnp.int32)
        return z if a == nz - 1 else jnp.where(z < nz // 2, low, high)

    def to_y(a, b):
        return rcopy(
            part.at[target(a) * ny + yo(b)], ry.at[a, b - 1], py_s.at[a, b], py_r.at[a, b], mpeer(z, yo(b))
        )

    for a in range(nz):
        for b in range(1, ny):
            partial(target(a) * ny + yo(b))
            go(to_y(a, b))
        if a < nz - 1:
            arrival(a + 1)

    @pl.loop(0, nz)
    def _(zz):
        partial(zz * ny + y)

    hid[...] = jnp.zeros_like(hid)

    def use(mm):
        am = act[mm].reshape(nd * tok, feat)
        for lo in range(0, ff, 256):
            hi = min(lo + 256, ff)
            wm = w[pl.ds(pl.multiple_of(mm * feat, feat), feat), lo:hi].astype(BF16)
            hid[:, :, lo:hi] += jnp.dot(am, wm, preferred_element_type=F32).reshape(nd, tok, hi - lo)
        flip[pl.ds(mm * local_blocks, local_blocks)] = am.T.astype(flip.dtype).reshape(
            local_blocks, width, nd * tok
        )

    def sum_y(a):
        mm = target(a) * ny + y
        for b in range(1, ny):
            to_y(a, b).wait_recv()

        @pl.loop(0, nd)
        def _(t):
            total = part[mm, t].astype(F32)
            for b in range(1, ny):
                total += ry[a, b - 1, t].astype(F32)
            part[mm, t] = total.astype(BF16)

    def to_z(zt):
        right = (zt > z).astype(jnp.int32)
        return rcopy(
            part.at[zt * ny + y], rz.at[1 - right, zt], pz_s.at[1 - right, zt], pz_r.at[1 - right, zt],
            mpeer(z + 2 * right - 1, y),
        )

    def from_z(side, zt):
        ref = rz.at[side, zt]
        rcopy(ref, ref, pz_s.at[side, zt], pz_r.at[side, zt], mpeer(z, y)).wait_recv()

    def sum_z(a):
        zt = target(a)
        side = 1 - (zt > z).astype(jnp.int32)
        sum_y(a)

        @pl.when(jnp.where(zt > z, z > 0, z < nz - 1))
        def _():
            from_z(side, zt)

            @pl.loop(0, nd)
            def _(t):
                part[zt * ny + y, t] = (
                    part[zt * ny + y, t].astype(F32) + rz[side, zt, t].astype(F32)
                ).astype(BF16)

        to_z(zt).start()

    def use_far(s):
        src = lax.rem(z + s, nz)
        for b in range(1, ny):
            across(src, b, True).wait_recv()
            use(src * ny + yo(-b))

    sum_z(0)

    @pl.loop(0, nz)
    def _(zz):
        use(zz * ny + y)

    sum_z(1)

    @pl.loop(0, nz)
    def _(s):
        use_far(s)

    @pl.loop(0, nd)
    def _(t):
        hsend[t] = hid[t].astype(BF16)

    hid_sent = [
        go(rcopy(hsend.at[lax.rem(d + o, nd)], hrecv.at[o - 1], hd_s.at[o], hd_r.at[o], dpeer(o)))
        for o in range(1, nd)
    ]
    saves = []
    order = lax.broadcasted_iota(jnp.int32, (slots, width, blk), 0)

    def block_grad(c):
        for k in range(slots):
            picked[k * width:(k + 1) * width, :] = flip[rows_ref[c, k]]
        got = jnp.dot(
            picked[...].astype(BF16), gall[:, :, c * blk:(c + 1) * blk].reshape(nd * tok, blk),
            preferred_element_type=F32,
        ).reshape(slots, width, blk)
        gv[c] = jnp.where(order < count_ref[c], got, 0.0).astype(gv.dtype)
        saves.append(pltpu.make_async_copy(gv.at[c], gv_hbm.at[c], gv_s.at[c]))
        saves[-1].start()

    for a in range(2, nz - 1):
        sum_z(a)
    for c in range(cols // 2):
        block_grad(c)
    sum_y(nz - 1)

    @pl.loop(0, nd)
    def _(t):
        tot[t] = part[m, t].astype(F32)

    for side in range(2):
        @pl.when(z > 0 if side == 0 else z < nz - 1)
        def _():
            from_z(side, z)

            @pl.loop(0, nd)
            def _(t):
                tot[t] += rz[side, z, t].astype(F32)

    @pl.loop(0, nd)
    def _(t):
        gasend[t] = tot[t].astype(BF16)

    garecv[d] = gasend[d]

    ga_sent = [
        go(rcopy(gasend.at[lax.rem(d + o, nd)], garecv.at[d], ga_s.at[o], ga_r.at[o], dpeer(o)))
        for o in range(1, nd)
    ]

    for c in range(cols // 2, cols):
        block_grad(c)

    for c in hid_sent:
        c.wait_recv()
    total = hid[d]
    for o in range(1, nd):
        total += hrecv[o - 1].astype(F32)
    hid_out[...] = total.astype(BF16)

    for c in ga_sent:
        c.wait_recv()
    for q in range(n_group):
        total = jnp.zeros((tok, group * blk), F32)
        for dd in range(nd):
            total += lax.dot_general(
                garecv[dd, :, q * gw:(q + 1) * gw], picks[dd], (((1,), (1,)), ((), ())),
                preferred_element_type=F32,
            )
        ga_out[:, q * group * blk:(q + 1) * group * blk] = total.astype(BF16)

    for c in saves:
        c.wait()
    for c in sends:
        c.wait_send()
    for src in range(nz):
        for b in range(1, ny):
            across(src, b, False).wait_send()

        @pl.when((z < nz - 1) & (z >= src))
        def _():
            along(True, src).wait_send()

        @pl.when((z > 0) & (z <= src))
        def _():
            along(False, src).wait_send()
    for a in range(nz - 1):
        to_z(target(a)).wait_send()


def shards(nd, nm, acts, grad_out, values, block_rows, block_count):
    tok, local = acts.shape
    ff = grad_out.shape[1]
    cols, slots, width, blk = values.shape
    nz = N_Z
    ny = nm // nz
    local_blocks = local // blk
    feat = local_blocks * width
    row_blocks = local_blocks * nm
    depth = feat * nm
    group = min(local_blocks, blk // width)
    if width % 16:
        values = values.astype(F32)
    kind = values.dtype
    slot_rows = -(-cols // 8) * 8
    slot_lanes = -(-row_blocks // 128) * 128
    dma = pltpu.SemaphoreType.DMA
    vmem = pl.BlockSpec(memory_space=pltpu.VMEM)
    smem = pl.BlockSpec(memory_space=pltpu.SMEM)
    hidden_out, grad_acts, grad_values = pl.pallas_call(
        functools.partial(kernel, nd, nm),
        out_shape=(
            jax.ShapeDtypeStruct((tok, ff), BF16),
            jax.ShapeDtypeStruct((tok, local), BF16),
            jax.ShapeDtypeStruct(values.shape, kind),
        ),
        in_specs=[smem] * 2 + [vmem] * 2 + [pl.BlockSpec(memory_space=pl.ANY)],
        out_specs=(vmem, vmem, pl.BlockSpec(memory_space=pl.ANY)),
        scratch_shapes=[
            pltpu.VMEM((slot_rows, slot_lanes), jnp.int32),
            pltpu.SMEM((slot_rows, slot_lanes), jnp.int32),
            pltpu.VMEM((cols, slots + 1, width, blk), kind),
            pltpu.VMEM((depth, ff), kind),
            pltpu.VMEM((row_blocks, width, nd * tok), kind),
            pltpu.VMEM((nd, tok, ff), BF16),
            pltpu.VMEM((slots * width, nd * tok), kind),
            pltpu.VMEM((nd, group * blk, group * width), BF16),
            pltpu.VMEM(values.shape, kind),
            pltpu.VMEM((nd, tok, feat), BF16),
            pltpu.VMEM((nm, nd, tok, feat), BF16),
            pltpu.VMEM((nm, nd, tok, feat), BF16),
            pltpu.VMEM((nz, ny - 1, nd, tok, feat), BF16),
            pltpu.VMEM((2, nz, nd, tok, feat), BF16),
            pltpu.VMEM((nd, tok, ff), F32),
            pltpu.VMEM((nd, tok, ff), BF16),
            pltpu.VMEM((nd - 1, tok, ff), BF16),
            pltpu.VMEM((nd, tok, feat), F32),
            pltpu.VMEM((nd, tok, feat), BF16),
            pltpu.VMEM((nd, tok, feat), BF16),
            dma(()), dma(()), dma((cols,)),
            dma((nd,)), dma((nd,)), dma((nd,)), dma((nd,)), dma((nd,)), dma((nd,)),
            dma((2, nz)), dma((2, nz)), dma((nz, ny)), dma((nz, ny)),
            dma((nz, ny)), dma((nz, ny)), dma((2, nz)), dma((2, nz)),
            dma((nd,)), dma((nd,)), dma((nd,)), dma((nd,)),
        ],
        compiler_params=pltpu.CompilerParams(
            collective_id=0, has_side_effects=True, vmem_limit_bytes=62 * 2 ** 20
        ),
        cost_estimate=pl.CostEstimate(
            flops=4 * nd * tok * depth * ff, bytes_accessed=2 ** 23, transcendentals=0
        ),
    )(block_rows, block_count, acts, grad_out, values)
    return hidden_out, grad_acts, grad_values.astype(F32)


def solution(mesh):
    placed = (P("dp", "mp"), P("dp", "mp"), P("mp", None, "dp", None), P("mp", None), P("mp"))
    return jax.shard_map(
        functools.partial(shards, mesh.shape["dp"], mesh.shape["mp"]),
        mesh=mesh,
        in_specs=placed,
        out_specs=(P("dp", "mp"), P("dp", "mp"), P("mp", None, "dp", None)),
        check_vma=False,
    )
```

```python
import functools

import jax
import jax.numpy as jnp
from jax import lax
from jax.experimental import pallas as pl
from jax.experimental.pallas import tpu as pltpu
from jax.sharding import PartitionSpec as P

MESH = pl.DeviceIdType.MESH
BF16 = jnp.bfloat16
F32 = jnp.float32
N_Z = 4


def select(rows_in, lanes, width, shift):
    src = lax.broadcasted_iota(jnp.int32, (rows_in, lanes), 0)
    dst = lax.broadcasted_iota(jnp.int32, (rows_in, lanes), 1)
    hit = src == (dst // width) * 128 + shift + dst % width
    return jnp.where(hit, 1.0, 0.0).astype(BF16)


def kernel(
    nd, nm,
    rows_ref, count_ref, acts_ref, gout_ref, val_hbm,
    hid_out, ga_out, gv_hbm,
    slot_v, slot_ref, val, w, flip, gall, picked, picks, gv,
    perm, act, part, ry, rz, hid, hsend, hrecv, tot, gasend, garecv,
    val_s, slot_s, gv_s, aa_s, aa_r, go_s, go_r, gf_s, gf_r, az_s, az_r, ay_s, ay_r,
    py_s, py_r, pz_s, pz_r, hd_s, hd_r, ga_s, ga_r,
):
    nz = N_Z
    ny = nm // nz
    half = nd // 2
    d = lax.axis_index("dp")
    m = lax.axis_index("mp")
    z = m // ny
    y = m % ny
    h = d // 2
    core = d % 2
    twin = (h * 2 + 1 - core, m)
    tok, local = acts_ref.shape
    ff = gout_ref.shape[1]
    cols, slots, width, blk = val_hbm.shape
    feat = act.shape[3]
    local_blocks = local // blk
    group = min(local_blocks, blk // width)
    gw = group * width
    n_group = local_blocks // group
    row_blocks = local_blocks * nm

    def dpeer(o):
        return (lax.rem(d + o, nd), m)

    def hpeer(o):
        return (lax.rem(h + o, half) * 2 + core, m)

    def mpeer(zz, yy):
        return (d, zz * ny + yy)

    def yo(o):
        return lax.rem(y + o + ny, ny)

    def rcopy(src, dst, ss, rs, dev):
        return pltpu.make_async_remote_copy(
            src_ref=src, dst_ref=dst, send_sem=ss, recv_sem=rs, device_id=dev, device_id_type=MESH
        )

    load = pltpu.make_async_copy(val_hbm, val.at[:, 0:slots], val_s)
    load.start()

    barrier = pltpu.get_barrier_semaphore()
    peers = [dpeer(o) for o in range(1, nd)]
    peers += [mpeer(z, yo(b)) for b in range(1, ny)]

    def greet(peer):
        pl.semaphore_signal(barrier, inc=1, device_id=peer, device_id_type=MESH)

    for peer in peers:
        greet(peer)

    @pl.when(z > 0)
    def _():
        greet(mpeer(z - 1, y))

    @pl.when(z < nz - 1)
    def _():
        greet(mpeer(z + 1, y))

    for dd in range(nd):
        picks[dd] = select(group * blk, gw, width, dd * width)
        for q in range(n_group):
            got = jnp.dot(
                acts_ref[:, q * group * blk:(q + 1) * group * blk], picks[dd], preferred_element_type=F32
            )
            perm[dd, :, q * gw:(q + 1) * gw] = got.astype(BF16)

    lane = lax.broadcasted_iota(jnp.int32, (1, slot_v.shape[1]), 1)
    slot_v[...] = jnp.zeros_like(slot_v)
    for c in range(cols):
        found = jnp.full(lane.shape, slots, jnp.int32)
        for k in range(slots):
            row = jnp.where(k < count_ref[c], rows_ref[c, k], -1)
            found = jnp.where(lane == row, k, found)
        slot_v[c:c + 1, :] = found
    to_scalar = pltpu.make_async_copy(slot_v, slot_ref, slot_s)
    to_scalar.start()

    ends = (z == 0).astype(jnp.int32) + (z == nz - 1).astype(jnp.int32)
    pl.semaphore_wait(barrier, len(peers) + 2 - ends)

    sends = []

    def go(c):
        c.start()
        sends.append(c)
        return c

    acts_sent = [
        go(rcopy(perm.at[lax.rem(d + o, nd)], act.at[m, d], aa_s.at[o], aa_r.at[o], dpeer(o)))
        for o in range(1, nd)
    ]
    gout_sent = [
        go(rcopy(gout_ref, gall.at[d], go_s.at[o], go_r.at[o], hpeer(o))) for o in range(1, half)
    ]
    gout_twin = [go(rcopy(gout_ref, gall.at[d], gf_s.at[0], gf_r.at[0], twin))]
    act[m, d] = perm[d]
    gall[d] = gout_ref[...]

    for c in acts_sent:
        c.wait_recv()

    def along(right, src):
        ref = act.at[src * ny + y]
        side = 0 if right else 1
        return rcopy(ref, ref, az_s.at[side, src], az_r.at[side, src], mpeer(z + 1 if right else z - 1, y))

    def across(src, b, back):
        ref = act.at[src * ny + (yo(-b) if back else y)]
        return rcopy(ref, ref, ay_s.at[src, b], ay_r.at[src, b], mpeer(z, yo(b)))

    def spread(src):
        for b in range(1, ny):
            across(src, b, False).start()

    @pl.when(z < nz - 1)
    def _():
        along(True, z).start()

    @pl.when(z > 0)
    def _():
        along(False, z).start()

    spread(z)

    load.wait()
    to_scalar.wait()
    for c in range(cols):
        val[c, slots] = jnp.zeros((width, blk), val.dtype)

    @pl.loop(0, row_blocks, unroll=2)
    def _(r):
        for c in range(cols):
            w[pl.ds(pl.multiple_of(r * width, width), width), c * blk:(c + 1) * blk] = val[
                c, slot_ref[c, r]
            ]

    def arrival(s):
        @pl.when(z >= s)
        def _():
            along(True, z - s).wait_recv()

            @pl.when(z < nz - 1)
            def _():
                along(True, z - s).start()

            spread(z - s)

        @pl.when(z + s < nz)
        def _():
            along(False, z + s).wait_recv()

            @pl.when(z > 0)
            def _():
                along(False, z + s).start()

            spread(z + s)

    for o, c in enumerate(gout_sent):
        c.wait_recv()
        ref = gall.at[lax.rem(h - (o + 1) + half, half) * 2 + core]
        gout_twin.append(go(rcopy(ref, ref, gf_s.at[o + 1], gf_r.at[o + 1], twin)))
    for c in gout_twin:
        c.wait_recv()

    def weights(mm):
        return w[pl.ds(pl.multiple_of(mm * feat, feat), feat), :].astype(BF16)

    def partial(mm):
        part[mm] = lax.dot_general(
            gall[...].reshape(nd * tok, ff), weights(mm), (((1,), (1,)), ((), ())),
            preferred_element_type=F32,
        ).astype(BF16).reshape(nd, tok, feat)

    def target(a):
        down = nz - 1 - a
        low = down - (down <= z).astype(jnp.int32)
        high = a + (jnp.int32(a) >= z).astype(jnp.int32)
        return z if a == nz - 1 else jnp.where(z < nz // 2, low, high)

    def to_y(a, b):
        return rcopy(
            part.at[target(a) * ny + yo(b)], ry.at[a, b - 1], py_s.at[a, b], py_r.at[a, b], mpeer(z, yo(b))
        )

    for a in range(nz):
        for b in range(1, ny):
            partial(target(a) * ny + yo(b))
            go(to_y(a, b))
        if a < nz - 1:
            arrival(a + 1)

    @pl.loop(0, nz)
    def _(zz):
        partial(zz * ny + y)

    hid[...] = jnp.zeros_like(hid)

    def use(mm):
        am = act[mm].reshape(nd * tok, feat)
        for lo in range(0, ff, 256):
            hi = min(lo + 256, ff)
            wm = w[pl.ds(pl.multiple_of(mm * feat, feat), feat), lo:hi].astype(BF16)
            hid[:, :, lo:hi] += jnp.dot(am, wm, preferred_element_type=F32).reshape(nd, tok, hi - lo)
        flip[pl.ds(mm * local_blocks, local_blocks)] = am.T.astype(flip.dtype).reshape(
            local_blocks, width, nd * tok
        )

    def sum_y(a):
        mm = target(a) * ny + y
        for b in range(1, ny):
            to_y(a, b).wait_recv()

        @pl.loop(0, nd)
        def _(t):
            total = part[mm, t].astype(F32)
            for b in range(1, ny):
                total += ry[a, b - 1, t].astype(F32)
            part[mm, t] = total.astype(BF16)

    def to_z(zt):
        right = (zt > z).astype(jnp.int32)
        return rcopy(
            part.at[zt * ny + y], rz.at[1 - right, zt], pz_s.at[1 - right, zt], pz_r.at[1 - right, zt],
            mpeer(z + 2 * right - 1, y),
        )

    def from_z(side, zt):
        ref = rz.at[side, zt]
        rcopy(ref, ref, pz_s.at[side, zt], pz_r.at[side, zt], mpeer(z, y)).wait_recv()

    def sum_z(a):
        zt = target(a)
        side = 1 - (zt > z).astype(jnp.int32)
        sum_y(a)

        @pl.when(jnp.where(zt > z, z > 0, z < nz - 1))
        def _():
            from_z(side, zt)

            @pl.loop(0, nd)
            def _(t):
                part[zt * ny + y, t] = (
                    part[zt * ny + y, t].astype(F32) + rz[side, zt, t].astype(F32)
                ).astype(BF16)

        to_z(zt).start()

    def use_far(s):
        src = lax.rem(z + s, nz)
        for b in range(1, ny):
            across(src, b, True).wait_recv()
            use(src * ny + yo(-b))

    sum_z(0)

    @pl.loop(0, nz)
    def _(zz):
        use(zz * ny + y)

    sum_z(1)

    @pl.loop(0, nz)
    def _(s):
        use_far(s)

    @pl.loop(0, nd)
    def _(t):
        hsend[t] = hid[t].astype(BF16)

    hid_sent = [
        go(rcopy(hsend.at[lax.rem(d + o, nd)], hrecv.at[o - 1], hd_s.at[o], hd_r.at[o], dpeer(o)))
        for o in range(1, nd)
    ]
    saves = []
    order = lax.broadcasted_iota(jnp.int32, (slots, width, blk), 0)

    def block_grad(c):
        for k in range(slots):
            picked[k * width:(k + 1) * width, :] = flip[rows_ref[c, k]]
        got = jnp.dot(
            picked[...].astype(BF16), gall[:, :, c * blk:(c + 1) * blk].reshape(nd * tok, blk),
            preferred_element_type=F32,
        ).reshape(slots, width, blk)
        gv[c] = jnp.where(order < count_ref[c], got, 0.0).astype(gv.dtype)
        saves.append(pltpu.make_async_copy(gv.at[c], gv_hbm.at[c], gv_s.at[c]))
        saves[-1].start()

    for a in range(2, nz - 1):
        sum_z(a)
    for c in range(cols // 2):
        block_grad(c)
    sum_y(nz - 1)

    @pl.loop(0, nd)
    def _(t):
        tot[t] = part[m, t].astype(F32)

    for side in range(2):
        @pl.when(z > 0 if side == 0 else z < nz - 1)
        def _():
            from_z(side, z)

            @pl.loop(0, nd)
            def _(t):
                tot[t] += rz[side, z, t].astype(F32)

    @pl.loop(0, nd)
    def _(t):
        gasend[t] = tot[t].astype(BF16)

    garecv[d] = gasend[d]

    ga_sent = [
        go(rcopy(gasend.at[lax.rem(d + o, nd)], garecv.at[d], ga_s.at[o], ga_r.at[o], dpeer(o)))
        for o in range(1, nd)
    ]

    for c in range(cols // 2, cols):
        block_grad(c)

    for c in hid_sent:
        c.wait_recv()
    total = hid[d]
    for o in range(1, nd):
        total += hrecv[o - 1].astype(F32)
    hid_out[...] = total.astype(BF16)

    for c in ga_sent:
        c.wait_recv()
    for q in range(n_group):
        total = jnp.zeros((tok, group * blk), F32)
        for dd in range(nd):
            total += lax.dot_general(
                garecv[dd, :, q * gw:(q + 1) * gw], picks[dd], (((1,), (1,)), ((), ())),
                preferred_element_type=F32,
            )
        ga_out[:, q * group * blk:(q + 1) * group * blk] = total.astype(BF16)

    for c in saves:
        c.wait()
    for c in sends:
        c.wait_send()
    for src in range(nz):
        for b in range(1, ny):
            across(src, b, False).wait_send()

        @pl.when((z < nz - 1) & (z >= src))
        def _():
            along(True, src).wait_send()

        @pl.when((z > 0) & (z <= src))
        def _():
            along(False, src).wait_send()
    for a in range(nz - 1):
        to_z(target(a)).wait_send()


def shards(nd, nm, acts, grad_out, values, block_rows, block_count):
    tok, local = acts.shape
    ff = grad_out.shape[1]
    cols, slots, width, blk = values.shape
    nz = N_Z
    ny = nm // nz
    local_blocks = local // blk
    feat = local_blocks * width
    row_blocks = local_blocks * nm
    depth = feat * nm
    group = min(local_blocks, blk // width)
    if width % 16:
        values = values.astype(F32)
    kind = values.dtype
    slot_rows = -(-cols // 8) * 8
    slot_lanes = -(-row_blocks // 128) * 128
    dma = pltpu.SemaphoreType.DMA
    vmem = pl.BlockSpec(memory_space=pltpu.VMEM)
    smem = pl.BlockSpec(memory_space=pltpu.SMEM)
    hidden_out, grad_acts, grad_values = pl.pallas_call(
        functools.partial(kernel, nd, nm),
        out_shape=(
            jax.ShapeDtypeStruct((tok, ff), BF16),
            jax.ShapeDtypeStruct((tok, local), BF16),
            jax.ShapeDtypeStruct(values.shape, kind),
        ),
        in_specs=[smem] * 2 + [vmem] * 2 + [pl.BlockSpec(memory_space=pl.ANY)],
        out_specs=(vmem, vmem, pl.BlockSpec(memory_space=pl.ANY)),
        scratch_shapes=[
            pltpu.VMEM((slot_rows, slot_lanes), jnp.int32),
            pltpu.SMEM((slot_rows, slot_lanes), jnp.int32),
            pltpu.VMEM((cols, slots + 1, width, blk), kind),
            pltpu.VMEM((depth, ff), kind),
            pltpu.VMEM((row_blocks, width, nd * tok), kind),
            pltpu.VMEM((nd, tok, ff), BF16),
            pltpu.VMEM((slots * width, nd * tok), kind),
            pltpu.VMEM((nd, group * blk, group * width), BF16),
            pltpu.VMEM(values.shape, kind),
            pltpu.VMEM((nd, tok, feat), BF16),
            pltpu.VMEM((nm, nd, tok, feat), BF16),
            pltpu.VMEM((nm, nd, tok, feat), BF16),
            pltpu.VMEM((nz, ny - 1, nd, tok, feat), BF16),
            pltpu.VMEM((2, nz, nd, tok, feat), BF16),
            pltpu.VMEM((nd, tok, ff), F32),
            pltpu.VMEM((nd, tok, ff), BF16),
            pltpu.VMEM((nd - 1, tok, ff), BF16),
            pltpu.VMEM((nd, tok, feat), F32),
            pltpu.VMEM((nd, tok, feat), BF16),
            pltpu.VMEM((nd, tok, feat), BF16),
            dma(()), dma(()), dma((cols,)),
            dma((nd,)), dma((nd,)), dma((nd,)), dma((nd,)), dma((nd,)), dma((nd,)),
            dma((2, nz)), dma((2, nz)), dma((nz, ny)), dma((nz, ny)),
            dma((nz, ny)), dma((nz, ny)), dma((2, nz)), dma((2, nz)),
            dma((nd,)), dma((nd,)), dma((nd,)), dma((nd,)),
        ],
        compiler_params=pltpu.CompilerParams(
            collective_id=0, has_side_effects=True, vmem_limit_bytes=62 * 2 ** 20
        ),
        cost_estimate=pl.CostEstimate(
            flops=4 * nd * tok * depth * ff, bytes_accessed=2 ** 23, transcendentals=0
        ),
    )(block_rows, block_count, acts, grad_out, values)
    return hidden_out, grad_acts, grad_values.astype(F32)


def solution(mesh):
    placed = (P("dp", "mp"), P("dp", "mp"), P("mp", None, "dp", None), P("mp", None), P("mp"))
    return jax.shard_map(
        functools.partial(shards, mesh.shape["dp"], mesh.shape["mp"]),
        mesh=mesh,
        in_specs=placed,
        out_specs=(P("dp", "mp"), P("dp", "mp"), P("mp", None, "dp", None)),
        check_vma=False,
    )
```
